32 devices in a mesh: slab: 4 (over y, core), tile: 8 (over z, x).
Axes of the slice: x: 2, y: 2, z: 4, core: 2. Of those that a mesh axis runs over, the one named last changes fastest.
Arguments:
- particles: float32 [8, 65536], P(None, ('slab', 'tile')), may hold values from -6 to 6, as said below
- halo_up: int32 [32], P(('slab', 'tile')), may hold values from 0 to 15
- halo_down: int32 [32], P(('slab', 'tile')), may hold values from 0 to 15
- tile_first: int32 [4, 1024], P('slab', 'tile'), may hold values from 0 to 127, as said below
- tile_second: int32 [4, 1024], P('slab', 'tile'), may hold values from 0 to 143
- tile_live: int32 [4, 1024], P('slab', 'tile'), may hold values from 0 to 1, as said below
- step_index: int32 [1], replicated, may hold values from 0 to 63
- time_step: float32 [1], replicated, may hold values from 0.05 to 0.5
Outputs:
- rates: float32 [4, 65536], P(None, ('slab', 'tile'))
- advanced: float32 [7, 65536], P(None, ('slab', 'tile'))
The draws below stay inside these ranges and needn't reach their ends.
Inputs may be any that keep to these rules, and one draw needn't show every extreme that they name: `particles`: densities lie between 0.85 and 1.15, masses between 0.0002 and 0.0008, positions between 0 and 3. `tile_first`: in each slab the 16 blocks of each device of the slab are named by exactly 128 of the slab's slots. `tile_live`: in each slab exactly half of the 1024 slots are live; how many fall on one device varies.
All inputs are finite; a program needn't handle non-finite values.
Results may differ from the reference program's by a relative error of at most 0.00018.
Values sent between devices are 32-bit elements; how exact they have to be, the bound alone decides.
No kernel may reach another device: no remote copies, remote signals or barrier semaphores. Data moves between devices by JAX's collectives and lax.ppermute only.
A program may use at most 64 MiB of HBM per device.

```python
import math
import jax
import jax.numpy as jnp
from jax import lax

PB = 128
BLK_DEV = 16
HALO_DEV = 1
TILE_DEV = 128
EXT_BLOCKS = 144
TILES_SLAB = 1024
PARTICLES = 65536
N_SLAB = 4
N_TILE = 8
DEVICES = 32


def draw_particles(key, part):
    subkeys = jax.random.split(key, 5)
    block_count = PARTICLES // PB
    centres = jax.random.uniform(subkeys[0], (3, block_count, 1), jnp.float32, 0.0, 2.0)
    offsets = jax.random.uniform(subkeys[1], (3, block_count, PB), jnp.float32, 0.0, 1.0)
    position = (centres + offsets).reshape(3, PARTICLES)
    velocity = jnp.clip(jax.random.normal(subkeys[2], (3, PARTICLES), jnp.float32), -4.0, 4.0)
    density = jax.random.uniform(subkeys[3], (1, PARTICLES), jnp.float32, 0.9, 1.1)
    masses = jnp.exp(jax.random.uniform(subkeys[4], (1, PARTICLES), jnp.float32, math.log(0.0002), math.log(0.0008)))
    return jnp.concatenate([position, velocity, density, masses], axis=0)


def draw_tile_first(key, part):
    subkeys = jax.random.split(jax.random.fold_in(key, 29), N_SLAB + 1)
    holders = jnp.repeat(jnp.arange(N_TILE, dtype=jnp.int32), TILE_DEV)
    within = jax.random.randint(subkeys[0], (N_SLAB, TILES_SLAB), 0, BLK_DEV)
    orders = jax.vmap(lambda one_key: jax.random.permutation(one_key, TILES_SLAB))(subkeys[1:])
    return (holders[orders] * BLK_DEV + within).astype(jnp.int32)


def draw_tile_live(key, part):
    subkeys = jax.random.split(jax.random.fold_in(key, 17), 2)
    per_device = TILES_SLAB // N_TILE
    leaning = jax.random.randint(subkeys[0], (N_SLAB, N_TILE, 1), 0, 4)
    leaning = jnp.broadcast_to(leaning, (N_SLAB, N_TILE, per_device)).reshape(N_SLAB, TILES_SLAB)
    jitter = jax.random.randint(subkeys[1], (N_SLAB, TILES_SLAB), 0, 1048576)
    scores = leaning * 1048576 + jitter
    ordering = jnp.argsort(-scores, axis=1, stable=True)
    ranking = jnp.argsort(ordering, axis=1, stable=True)
    return (ranking < TILES_SLAB // 2).astype(jnp.int32)


def touch_ends(entries, own_key, smallest, top_value):
    place = [jax.random.randint(jax.random.fold_in(own_key, axis), (), 0, length) for axis, length in enumerate(entries.shape)]
    widest = entries.shape.index(max(entries.shape))
    beside = place[:widest] + [(place[widest] + 1) % entries.shape[widest]] + place[widest + 1:]
    return entries.at[tuple(place)].set(smallest).at[tuple(beside)].set(top_value)


def setup_inputs(seed: int = 0) -> dict:
    splits = jax.random.split(jax.random.key(seed), 9)
    return {
        "particles": draw_particles(jax.random.fold_in(splits[8], 71), 0),
        "halo_up": touch_ends(jax.random.randint(splits[1], (HALO_DEV * DEVICES,), 0, BLK_DEV), jax.random.fold_in(splits[1], 1), 0, BLK_DEV - 1).astype(jnp.int32),
        "halo_down": touch_ends(jax.random.randint(splits[2], (HALO_DEV * DEVICES,), 0, BLK_DEV), jax.random.fold_in(splits[2], 1), 0, BLK_DEV - 1).astype(jnp.int32),
        "tile_first": draw_tile_first(jax.random.fold_in(splits[8], 71), 0),
        "tile_second": touch_ends(jax.random.randint(splits[4], (N_SLAB, TILES_SLAB), 0, EXT_BLOCKS), jax.random.fold_in(splits[4], 1), 0, EXT_BLOCKS - 1).astype(jnp.int32),
        "tile_live": draw_tile_live(jax.random.fold_in(splits[8], 71), 0),
        "step_index": jax.random.randint(splits[6], (1,), 0, 64).astype(jnp.int32),
        "time_step": jnp.clip(jnp.exp(jax.random.uniform(splits[7], (1,), jnp.float32, math.log(0.05), math.log(0.5))), 0.05, 0.5),
    }


SMOOTHING = 1.0
KERNEL_NORM = 21.0 / (16.0 * 3.141592653589793)
SOUND_SPEED = 10.0
STIFFNESS = SOUND_SPEED * SOUND_SPEED / 7.0
VISCOSITY = 0.1
BLAST_STRENGTH = 8.0
DECAY_TIME = 8.0

def carried_fields(particles):
    density = particles[6]
    pressure = STIFFNESS * (density ** 7 - 1.0)
    return jnp.concatenate([particles[0:6], particles[7:8], (pressure / (density * density))[None], density[None]], axis=0)

def pair_terms(owned_block, neighbour):
    offsets = owned_block[0:3, :, :, None] - neighbour[0:3, :, None, :]
    dist_sq = lax.optimization_barrier(jnp.sum(offsets * offsets, axis=0))
    support = jnp.maximum(1.0 - jnp.sqrt(dist_sq) / (2.0 * SMOOTHING), 0.0)
    gradient = -5.0 * KERNEL_NORM * support ** 3 / SMOOTHING ** 5
    approach = lax.optimization_barrier(jnp.sum((owned_block[3:6, :, :, None] - neighbour[3:6, :, None, :]) * offsets, axis=0))
    masses = neighbour[6][:, None, :]
    density_rate = lax.optimization_barrier(jnp.sum(masses * approach * gradient, axis=2))
    mean_density = 0.5 * (owned_block[8][:, :, None] + neighbour[8][:, None, :])
    damping = -VISCOSITY * SOUND_SPEED * SMOOTHING * jnp.minimum(approach, 0.0) / ((dist_sq + 0.01 * SMOOTHING * SMOOTHING) * mean_density)
    pressing = -masses * (owned_block[7][:, :, None] + neighbour[7][:, None, :] + damping) * gradient
    forcing = lax.optimization_barrier(jnp.sum(pressing[None] * offsets, axis=3))
    return jnp.concatenate([density_rate[None], forcing], axis=0)

def finish(particles, tile_rates, step_index, time_step):
    step_length = time_step[0]
    elapsed = step_index[0].astype(particles.dtype) * step_length
    strength = BLAST_STRENGTH * jnp.exp(-elapsed / DECAY_TIME)
    relative = particles[0:3] + 1.0
    spread_sq = lax.optimization_barrier(jnp.sum(relative * relative, axis=0)) + 1.0
    source = strength * relative / (spread_sq * jnp.sqrt(spread_sq))
    forcing = tile_rates[1:4] + source
    rates = jnp.concatenate([tile_rates[0:1], forcing], axis=0)
    velocity = particles[3:6] + step_length * forcing
    position = particles[0:3] + step_length * velocity
    density = particles[6:7] + step_length * tile_rates[0:1]
    return (rates, jnp.concatenate([position, velocity, density], axis=0))

def slab_rates(slab_item):
    extended, first_ids, second_ids, live_flags = slab_item
    batch_size = TILE_DEV
    turn_count = first_ids.shape[0] // batch_size
    scales = live_flags.astype(extended.dtype)

    def accumulate(running, batch_item):
        owned_ids, other_ids, weights = batch_item
        owned_block = jnp.take(extended, owned_ids, axis=1)
        neighbour = jnp.take(extended, other_ids, axis=1)
        pair_sums = pair_terms(owned_block, neighbour) * weights[None, :, None]
        running = running + jax.ops.segment_sum(jnp.moveaxis(pair_sums, 1, 0), owned_ids, num_segments=BLK_DEV * N_TILE)
        return (running, None)
    initial = jnp.zeros((BLK_DEV * N_TILE, 4, PB), extended.dtype)
    running, ignored = lax.scan(accumulate, initial, (first_ids.reshape(turn_count, batch_size), second_ids.reshape(turn_count, batch_size), scales.reshape(turn_count, batch_size)))
    return jnp.transpose(running, (1, 0, 2))

def reference(particles, halo_up, halo_down, tile_first, tile_second, tile_live, step_index, time_step):
    carried = carried_fields(particles)
    blocks = carried.reshape(9, N_SLAB, N_TILE, BLK_DEV, PB)

    def chosen(indices):
        pick_index = jnp.broadcast_to(indices.astype(jnp.int32).reshape(1, N_SLAB, N_TILE, HALO_DEV, 1), (9, N_SLAB, N_TILE, HALO_DEV, PB))
        return jnp.take_along_axis(blocks, pick_index, axis=3).reshape(9, N_SLAB, N_TILE * HALO_DEV, PB)
    sent_up = chosen(halo_up)
    sent_down = chosen(halo_down)
    empty_rim = jnp.zeros((9, 1, N_TILE * HALO_DEV, PB), carried.dtype)
    from_below = jnp.concatenate([empty_rim, sent_up[:, :-1]], axis=1)
    from_above = jnp.concatenate([sent_down[:, 1:], empty_rim], axis=1)
    owned_blocks = blocks.reshape(9, N_SLAB, BLK_DEV * N_TILE, PB)
    extended = jnp.concatenate([owned_blocks, from_below, from_above], axis=2)
    extended = jnp.transpose(extended, (1, 0, 2, 3))
    slab_sums = lax.map(slab_rates, (extended, tile_first, tile_second, tile_live))
    tile_rates = jnp.transpose(slab_sums, (1, 0, 2, 3)).reshape(4, -1)
    return finish(particles, tile_rates, step_index, time_step)
```

```python
import functools

import jax
import jax.numpy as jnp
from jax import lax
from jax.experimental import pallas as pl
from jax.experimental.pallas import tpu as pltpu
from jax.sharding import PartitionSpec as P

PB = 128
BLK_DEV = 16

SMOOTHING = 1.0
KERNEL_NORM = 21.0 / (16.0 * 3.141592653589793)
SOUND_SPEED = 10.0
STIFFNESS = SOUND_SPEED * SOUND_SPEED / 7.0
VISCOSITY = 0.1
BLAST_STRENGTH = 8.0
DECAY_TIME = 8.0

KAPPA = (5.0 * KERNEL_NORM) ** (1.0 / 3.0)
SCALE = 0.5 * KAPPA
SCALE_SQ = SCALE * SCALE
CENTRE = 1.5
UNROLL = 2
ROWS = 32

F32 = jnp.float32
BF16 = jnp.bfloat16
VMEM = pl.BlockSpec(memory_space=pltpu.VMEM)
SMEM = pl.BlockSpec(memory_space=pltpu.SMEM)
PARAMS = pltpu.CompilerParams(vmem_limit_bytes=48 * 1024 * 1024)


def split_3(value):
    first = value.astype(BF16).astype(F32)
    rest = value - first
    second = rest.astype(BF16).astype(F32)
    return first, second, (rest - second).astype(BF16).astype(F32)


def divided(value, by):
    if by & (by - 1) == 0:
        return lax.shift_right_logical(value, by.bit_length() - 1)
    return jnp.floor((value.astype(F32) + 0.5) * (1.0 / by)).astype(jnp.int32)


def pre_kernel(up_ids, down_ids, particles, first, second, live, pair_out, up_out, down_out):
    width = particles.shape[1]
    pair_out[:, 0:width] = particles[...]
    pair_out[:, width : width + PB] = jnp.zeros((8, PB), F32)
    for row, values in enumerate((first, second, live)):
        pair_out[row : row + 1, width : width + PB] = values[...].astype(F32)
    for ids, out in ((up_ids, up_out), (down_ids, down_out)):
        for item in range(out.shape[1] // PB):
            start = pl.multiple_of(ids[item] * PB, PB)
            out[:, item * PB : (item + 1) * PB] = particles[:, pl.ds(start, PB)]


def mid_kernel(pair, partner, below, above, column_out):
    width = pair.shape[1] - PB
    rim = below.shape[1]
    column_out[:, 0:width] = pair[:, 0:width]
    column_out[:, width : width + rim] = below[...]
    column_out[:, width + rim : width + 2 * rim] = above[...]
    column_out[:, width + 2 * rim :] = pair[:, width:]
    column_out[3:6, width + 2 * rim :] = partner[0:3, width:]


def pressure_term(density):
    term = STIFFNESS * (density**7 - 1.0) / (density * density)
    return jnp.where(density > 0.0, term, 0.0)


def pair_kernel(shifts, rim, *refs):
    columns = refs[:shifts]
    partner, own_out, other_out = refs[shifts : shifts + 3]
    acting, summing, receiving, raw_acting, raw_receiving, sums, products, parts, lists, codes, codes_smem, sem = refs[
        shifts + 3 :
    ]
    dev_blocks = BLK_DEV + 2 * rim
    tile = lax.axis_index("tile")
    row, column = lax.div(tile, 2), lax.rem(tile, 2)
    list_start = dev_blocks * PB
    holders = 2 * shifts
    slots = codes.shape[1]

    for shift in range(shifts):
        for side in range(2):
            for kind in range(3):
                lists[kind, 2 * shift + side : 2 * shift + side + 1, :] = columns[shift][
                    3 * side + kind : 3 * side + kind + 1, list_start : list_start + PB
                ]
    first = lists[0].astype(jnp.int32)
    second = lists[1].astype(jnp.int32)
    slab_blocks = holders * BLK_DEV
    is_rim = second >= slab_blocks
    rim_number = second - slab_blocks
    is_above = rim_number >= holders * rim
    rim_number = jnp.where(is_above, rim_number - holders * rim, rim_number)
    rim_owner = divided(rim_number, rim)
    owner = jnp.where(is_rim, rim_owner, divided(second, BLK_DEV))
    place = jnp.where(
        is_rim,
        BLK_DEV + rim_number - rim_owner * rim + jnp.where(is_above, rim, 0),
        second & (BLK_DEV - 1),
    )
    behind = row - divided(owner, 2)
    behind = jnp.where(behind < 0, behind + shifts, behind)
    target = divided(first, BLK_DEV)
    mine = (lists[2] > 0.5) & (divided(target, 2) == row) & ((owner & 1) == column)
    receiver = (first & (BLK_DEV - 1)) + jnp.where((target & 1) == column, 0, BLK_DEV)
    code = receiver * 1024 + behind * dev_blocks + place
    chosen = jnp.where(mine, 1.0, 0.0)
    lane = lax.broadcasted_iota(jnp.int32, (PB, PB), 1)
    sublane = lax.broadcasted_iota(jnp.int32, (PB, PB), 0)
    earlier = jnp.where(sublane < lane, 1.0, 0.0).astype(BF16)
    rank = jnp.dot(chosen.astype(BF16), earlier, preferred_element_type=F32)
    counts = jnp.sum(chosen, axis=1, keepdims=True)
    offset = jnp.zeros((1, 1), F32)
    offsets = []
    for holder in range(holders):
        offsets.append(offset)
        offset = offset + counts[holder : holder + 1]
    rank = rank + jnp.concatenate(offsets, axis=0)
    count = jnp.max(offset).astype(jnp.int32)
    rank = jnp.where(mine, rank.astype(jnp.int32), -1)
    dummy = 2 * BLK_DEV * 1024
    spread = lax.broadcasted_iota(jnp.int32, (PB, slots), 1)
    rank_t = jnp.transpose(jnp.concatenate([rank, jnp.zeros((PB - holders, PB), jnp.int32)], axis=0))
    code_t = jnp.transpose(
        jnp.concatenate([code - dummy, jnp.zeros((PB - holders, PB), jnp.int32)], axis=0)
    )
    found = jnp.zeros((8, slots), jnp.int32)
    for holder in range(holders):
        placed = jnp.where(
            rank_t[:, holder : holder + 1] == spread, code_t[:, holder : holder + 1], 0
        )
        for start in range(0, PB, 8):
            found = found + placed[start : start + 8]
    codes[...] = jnp.broadcast_to(jnp.sum(found, axis=0, keepdims=True) + dummy, codes.shape)
    copy = pltpu.make_async_copy(codes, codes_smem, sem)
    copy.start()

    row_8 = lax.broadcasted_iota(jnp.int32, (8, PB), 0)
    one = jnp.ones((1, PB), F32)
    none = jnp.zeros((1, PB), F32)

    def fields(block):
        spot = block[0:3] - CENTRE
        scaled = spot * SCALE
        speed = block[3:6]
        norm = jnp.sum(scaled * scaled, axis=0, keepdims=True)
        inner = jnp.sum(spot * speed, axis=0, keepdims=True)
        return spot, scaled, speed, norm, inner, block[6:7], block[7:8]

    def prepare_receiving(number, block):
        spot, scaled, speed, norm, inner, density, mass = fields(block)
        near = split_3(jnp.concatenate([scaled, norm, one, none, none, none], axis=0))
        meet = split_3(jnp.concatenate([speed, spot, inner, one], axis=0))
        order = (0, 0, 1, 1, 0, 2)
        extra = jnp.concatenate(
            [pressure_term(density), density * (-0.5 / SCALE_SQ), jnp.zeros((30, PB), F32)], axis=0
        )
        stacked = jnp.concatenate([near[k] for k in order] + [meet[k] for k in order] + [extra], axis=0)
        turned = jnp.transpose(stacked)
        receiving[number] = turned.astype(BF16)
        raw_receiving[number, 0] = jnp.broadcast_to(turned[:, 96:97], (PB, PB))
        raw_receiving[number, 1] = jnp.broadcast_to(turned[:, 97:98], (PB, PB))

    def prepare_acting(number, block):
        spot, scaled, speed, norm, inner, density, mass = fields(block)
        near = split_3(jnp.concatenate([-2.0 * scaled, one, norm, none, none, none], axis=0))
        meet = split_3(jnp.concatenate([-spot, -speed, one, inner], axis=0))
        order = (0, 1, 0, 1, 2, 0)
        empty = jnp.zeros((48, PB), BF16)
        acting[number, 0:48, 0:PB] = jnp.concatenate([near[k] for k in order], axis=0).astype(BF16)
        acting[number, 0:48, PB:] = empty
        acting[number, 48:96, 0:PB] = empty
        acting[number, 48:96, PB:] = jnp.concatenate([meet[k] for k in order], axis=0).astype(BF16)
        weighted = split_3(jnp.concatenate([mass, mass * spot, none, none, none, none], axis=0))
        blank = jnp.zeros((8, PB), F32)
        summing[number, :, 0:PB] = jnp.concatenate([*weighted, blank], axis=0).astype(BF16)
        summing[number, :, PB:] = jnp.concatenate(
            [weighted[0], weighted[1], blank, blank], axis=0
        ).astype(BF16)
        raw_acting[number] = jnp.concatenate(
            [pressure_term(density), density * (-0.5 / SCALE_SQ), jnp.zeros((6, PB), F32)], axis=0
        )

    def block_at(ref, number):
        return ref[:, pl.ds(pl.multiple_of(number * PB, PB), PB)]

    def each_receiving(number, carry):
        prepare_receiving(number, block_at(columns[0], number))
        prepare_receiving(number + BLK_DEV, block_at(partner, number))
        return carry

    lax.fori_loop(0, BLK_DEV, each_receiving, 0)
    receiving[2 * BLK_DEV] = jnp.zeros((PB, PB), BF16)
    raw_receiving[2 * BLK_DEV] = jnp.ones((2, PB, PB), F32)

    def each_acting(number, carry):
        for shift in range(shifts):
            prepare_acting(shift * dev_blocks + number, block_at(columns[shift], number))
        return carry

    lax.fori_loop(0, dev_blocks, each_acting, 0)
    sums[...] = jnp.zeros(sums.shape, F32)
    copy.wait()

    def work(turn, carry):
        for lot in range(UNROLL):
            item = codes_smem[0, turn * UNROLL + lot]
            target_number = lax.shift_right_logical(item, 10)
            source_number = item & 1023
            products[lot] = jnp.dot(
                receiving[target_number, :, 0:96],
                acting[source_number],
                preferred_element_type=F32,
            )
            pressure_row = raw_acting[source_number, 0:1, :]
            density_row = raw_acting[source_number, 1:2, :]
            for start in range(0, PB, ROWS):
                span = slice(start, start + ROWS)
                dist_sq = jnp.maximum(products[lot, span, 0:PB], 1e-12)
                approach = products[lot, span, PB:]
                support = jnp.maximum(KAPPA - dist_sq * lax.rsqrt(dist_sq), 0.0)
                gradient = support * support * support
                closing = approach * gradient
                weight = (dist_sq + 0.01 * SCALE_SQ) * (
                    raw_receiving[target_number, 1, span, :] + density_row
                )
                damping = jnp.minimum(approach, 0.0) * pl.reciprocal(weight, approx=True)
                pressing = (
                    raw_receiving[target_number, 0, span, :] + pressure_row + damping
                ) * gradient
                for base, value in ((0, pressing), (PB, closing)):
                    high = value.astype(BF16)
                    low = (value - high.astype(F32)).astype(BF16)
                    rows = slice(base + start, base + start + ROWS)
                    parts[lot, rows, 0:PB] = high
                    parts[lot, rows, PB:] = low
            total = lax.dot_general(
                summing[source_number],
                parts[lot],
                (((1,), (1,)), ((), ())),
                preferred_element_type=F32,
            )
            sums[target_number] += total[0:8] + total[8:16] + total[16:24]
        return carry

    lax.fori_loop(0, lax.div(count + UNROLL - 1, UNROLL), work, 0)

    def each_result(number, carry):
        start = pl.multiple_of(number * PB, PB)
        for base, source, out in ((0, columns[0], own_out), (BLK_DEV, partner, other_out)):
            total = sums[number + base]
            spot = source[0:3, pl.ds(start, PB)] - CENTRE
            force = spot * total[0:1, 0:PB] - total[1:4, 0:PB]
            out[0:1, pl.ds(start, PB)] = -total[0:1, PB:]
            out[1:4, pl.ds(start, PB)] = force
        return carry

    lax.fori_loop(0, BLK_DEV, each_result, 0)


def finish_kernel(step_index, time_step, particles, own, other, rates_out, advanced_out):
    step_length = time_step[0]
    elapsed = step_index[0].astype(F32) * step_length
    strength = BLAST_STRENGTH * jnp.exp(jnp.full((1, PB), -elapsed / DECAY_TIME, F32))[:, 0:1]
    block = particles[...]
    tile_rates = own[...] + other[...]
    relative = block[0:3] + 1.0
    spread_sq = jnp.sum(relative * relative, axis=0, keepdims=True) + 1.0
    source = strength * relative / (spread_sq * jnp.sqrt(spread_sq))
    forcing = tile_rates[1:4] + source
    rates_out[0:1] = tile_rates[0:1]
    rates_out[1:4] = forcing
    velocity = block[3:6] + step_length * forcing
    advanced_out[0:3] = block[0:3] + step_length * velocity
    advanced_out[3:6] = velocity
    advanced_out[6:7] = block[6:7] + step_length * tile_rates[0:1]


def on_device(
    particles, halo_up, halo_down, tile_first, tile_second, tile_live, step_index, time_step
):
    width = particles.shape[1]
    rim = halo_up.shape[0]
    rim_width = rim * PB
    tiles, slabs = lax.axis_size("tile"), lax.axis_size("slab")
    shifts = tiles // 2
    dev_blocks = BLK_DEV + 2 * rim
    pair, sent_up, sent_down = pl.pallas_call(
        pre_kernel,
        out_shape=(
            jax.ShapeDtypeStruct((8, width + PB), F32),
            jax.ShapeDtypeStruct((8, rim_width), F32),
            jax.ShapeDtypeStruct((8, rim_width), F32),
        ),
        in_specs=[SMEM, SMEM, VMEM, VMEM, VMEM, VMEM],
        out_specs=(VMEM, VMEM, VMEM),
        name="pack",
    )(halo_up, halo_down, particles, tile_first, tile_second, tile_live)
    across = [(i, i ^ 1) for i in range(tiles)]
    partner = lax.ppermute(pair, "tile", across)
    below = lax.ppermute(sent_up, "slab", [(i, i + 1) for i in range(slabs - 1)])
    above = lax.ppermute(sent_down, "slab", [(i + 1, i) for i in range(slabs - 1)])
    column = pl.pallas_call(
        mid_kernel,
        out_shape=jax.ShapeDtypeStruct((8, width + 2 * rim_width + PB), F32),
        in_specs=[VMEM] * 4,
        out_specs=VMEM,
        name="join",
    )(pair, partner, below, above)
    columns = [column]
    for shift in range(1, shifts):
        ring = [(i, (i + 2 * shift) % tiles) for i in range(tiles)]
        columns.append(lax.ppermute(column, "tile", ring))
    receivers, actors = 2 * BLK_DEV + 1, shifts * dev_blocks
    slots = 2 * tile_first.shape[-1] + PB
    partial = jax.ShapeDtypeStruct((4, width), F32)
    own, other = pl.pallas_call(
        functools.partial(pair_kernel, shifts, rim),
        out_shape=(partial, partial),
        in_specs=[VMEM] * (shifts + 1),
        out_specs=(VMEM, VMEM),
        scratch_shapes=[
            pltpu.VMEM((actors, 96, 2 * PB), BF16),
            pltpu.VMEM((actors, 32, 2 * PB), BF16),
            pltpu.VMEM((receivers, PB, PB), BF16),
            pltpu.VMEM((actors, 8, PB), F32),
            pltpu.VMEM((receivers, 2, PB, PB), F32),
            pltpu.VMEM((receivers, 8, 2 * PB), F32),
            pltpu.VMEM((UNROLL, PB, 2 * PB), F32),
            pltpu.VMEM((UNROLL, 2 * PB, 2 * PB), BF16),
            pltpu.VMEM((3, tiles, PB), F32),
            pltpu.VMEM((8, slots), jnp.int32),
            pltpu.SMEM((8, slots), jnp.int32),
            pltpu.SemaphoreType.DMA,
        ],
        compiler_params=PARAMS,
        name="pairs",
    )(*columns, partner)
    other = lax.ppermute(other, "tile", across)
    return pl.pallas_call(
        finish_kernel,
        out_shape=(
            jax.ShapeDtypeStruct((4, width), F32),
            jax.ShapeDtypeStruct((7, width), F32),
        ),
        in_specs=[SMEM, SMEM, VMEM, VMEM, VMEM],
        out_specs=(VMEM, VMEM),
        name="advance",
    )(step_index, time_step, particles, own, other)


def solution(mesh):
    placed = (
        P(None, ("slab", "tile")),
        P(("slab", "tile")),
        P(("slab", "tile")),
        P("slab", "tile"),
        P("slab", "tile"),
        P("slab", "tile"),
        P(),
        P(),
    )
    return jax.shard_map(
        on_device,
        mesh=mesh,
        in_specs=placed,
        out_specs=(P(None, ("slab", "tile")), P(None, ("slab", "tile"))),
        check_vma=False,
    )
```

```python
import functools

import jax
import jax.numpy as jnp
from jax import lax
from jax.experimental import pallas as pl
from jax.experimental.pallas import tpu as pltpu
from jax.sharding import PartitionSpec as P

PB = 128
BLK_DEV = 16

SMOOTHING = 1.0
KERNEL_NORM = 21.0 / (16.0 * 3.141592653589793)
SOUND_SPEED = 10.0
STIFFNESS = SOUND_SPEED * SOUND_SPEED / 7.0
VISCOSITY = 0.1
BLAST_STRENGTH = 8.0
DECAY_TIME = 8.0

KAPPA = (5.0 * KERNEL_NORM) ** (1.0 / 3.0)
SCALE = 0.5 * KAPPA
SCALE_SQ = SCALE * SCALE
CENTRE = 1.5
DENSITY_SCALE = -0.5 / (VISCOSITY * SOUND_SPEED * SMOOTHING * SCALE_SQ)
UNROLL = 8
ROWS = 32

F32 = jnp.float32
BF16 = jnp.bfloat16
VMEM = pl.BlockSpec(memory_space=pltpu.VMEM)
SMEM = pl.BlockSpec(memory_space=pltpu.SMEM)
PARAMS = pltpu.CompilerParams(vmem_limit_bytes=48 * 1024 * 1024)


def split_3(value):
    first = value.astype(BF16).astype(F32)
    rest = value - first
    second = rest.astype(BF16).astype(F32)
    return first, second, rest - second


def stacked(parts, order):
    return [parts[k] for k in order]


def divided(value, by):
    if by & (by - 1) == 0:
        return lax.shift_right_logical(value, by.bit_length() - 1)
    return jnp.floor((value.astype(F32) + 0.5) * (1.0 / by)).astype(jnp.int32)


def pre_kernel(up_ids, down_ids, particles, first, second, live, pair_out, up_out, down_out):
    width = particles.shape[1]
    pair_out[:, 0:width] = particles[...]
    pair_out[:, width : width + PB] = jnp.zeros((8, PB), F32)
    for row, values in enumerate((first, second, live)):
        pair_out[row : row + 1, width : width + PB] = values[...].astype(F32)
    for ids, out in ((up_ids, up_out), (down_ids, down_out)):
        for item in range(out.shape[1] // PB):
            start = pl.multiple_of(ids[item] * PB, PB)
            out[:, item * PB : (item + 1) * PB] = particles[:, pl.ds(start, PB)]


def mid_kernel(pair, partner, below, above, column_out):
    width = pair.shape[1] - PB
    rim = below.shape[1]
    column_out[:, 0:width] = pair[:, 0:width]
    column_out[:, width : width + rim] = below[...]
    column_out[:, width + rim : width + 2 * rim] = above[...]
    column_out[:, width + 2 * rim :] = pair[:, width:]
    column_out[3:6, width + 2 * rim :] = partner[0:3, width:]


def pressure_term(density):
    term = STIFFNESS * (density**7 - 1.0) / (density * density)
    return jnp.where(density > 0.0, term, 0.0)


def pair_kernel(shifts, rim, *refs):
    columns = refs[:shifts]
    partner, own_out, other_out = refs[shifts : shifts + 3]
    acting, summing, receiving, sums, products, parts, lists, codes, codes_smem, sem = refs[shifts + 3 :]
    dev_blocks = BLK_DEV + 2 * rim
    tile = lax.axis_index("tile")
    row, column = lax.div(tile, 2), lax.rem(tile, 2)
    list_start = dev_blocks * PB
    holders = 2 * shifts
    slots = codes.shape[1]

    for shift in range(shifts):
        for side in range(2):
            for kind in range(3):
                lists[kind, 2 * shift + side : 2 * shift + side + 1, :] = columns[shift][
                    3 * side + kind : 3 * side + kind + 1, list_start : list_start + PB
                ]
    first = lists[0].astype(jnp.int32)
    second = lists[1].astype(jnp.int32)
    slab_blocks = holders * BLK_DEV
    is_rim = second >= slab_blocks
    rim_number = second - slab_blocks
    is_above = rim_number >= holders * rim
    rim_number = jnp.where(is_above, rim_number - holders * rim, rim_number)
    rim_owner = divided(rim_number, rim)
    owner = jnp.where(is_rim, rim_owner, divided(second, BLK_DEV))
    place = jnp.where(
        is_rim,
        BLK_DEV + rim_number - rim_owner * rim + jnp.where(is_above, rim, 0),
        second & (BLK_DEV - 1),
    )
    behind = row - divided(owner, 2)
    behind = jnp.where(behind < 0, behind + shifts, behind)
    target = divided(first, BLK_DEV)
    mine = (lists[2] > 0.5) & (divided(target, 2) == row) & ((owner & 1) == column)
    receiver = (first & (BLK_DEV - 1)) + jnp.where((target & 1) == column, 0, BLK_DEV)
    code = receiver * 1024 + behind * dev_blocks + place
    chosen = jnp.where(mine, 1.0, 0.0)
    lane = lax.broadcasted_iota(jnp.int32, (PB, PB), 1)
    sublane = lax.broadcasted_iota(jnp.int32, (PB, PB), 0)
    earlier = jnp.where(sublane < lane, 1.0, 0.0).astype(BF16)
    rank = jnp.dot(chosen.astype(BF16), earlier, preferred_element_type=F32)
    counts = jnp.sum(chosen, axis=1, keepdims=True)
    offset = jnp.zeros((1, 1), F32)
    offsets = []
    for holder in range(holders):
        offsets.append(offset)
        offset = offset + counts[holder : holder + 1]
    rank = rank + jnp.concatenate(offsets, axis=0)
    count = jnp.max(offset).astype(jnp.int32)
    rank = jnp.where(mine, rank.astype(jnp.int32), -1)
    dummy = 2 * BLK_DEV * 1024
    spread = lax.broadcasted_iota(jnp.int32, (PB, slots), 1)
    rank_t = jnp.transpose(jnp.concatenate([rank, jnp.zeros((PB - holders, PB), jnp.int32)], axis=0))
    code_t = jnp.transpose(
        jnp.concatenate([code - dummy, jnp.zeros((PB - holders, PB), jnp.int32)], axis=0)
    )
    found = jnp.zeros((8, slots), jnp.int32)
    for holder in range(holders):
        placed = jnp.where(
            rank_t[:, holder : holder + 1] == spread, code_t[:, holder : holder + 1], 0
        )
        for start in range(0, PB, 8):
            found = found + placed[start : start + 8]
    codes[...] = jnp.broadcast_to(jnp.sum(found, axis=0, keepdims=True) + dummy, codes.shape)
    copy = pltpu.make_async_copy(codes, codes_smem, sem)
    copy.start()

    row_8 = lax.broadcasted_iota(jnp.int32, (8, PB), 0)
    centre = jnp.where(row_8 < 3, CENTRE, 0.0)
    scale = jnp.where(row_8 < 3, SCALE, 0.0)
    blank = jnp.zeros((8, PB), F32)

    def fields(block):
        moved = block - centre
        scaled = moved * scale
        norm = jnp.sum(scaled * scaled, axis=0, keepdims=True)
        inner = jnp.sum(moved[0:3] * moved[3:6], axis=0, keepdims=True)
        density = block[6:7]
        return moved, scaled, norm, inner, density * DENSITY_SCALE, pressure_term(density), block[7:8]

    def by_row(*rows):
        value = rows[-1]
        for row, other in zip(range(len(rows) - 2, -1, -1), rows[-2::-1]):
            value = jnp.where(row_8 == row, other, value)
        return value

    first_order, second_order = (0, 1, 0, 1, 2, 0), (0, 0, 1, 1, 0, 2)

    def columns_of(near, meet, rest, orders):
        rows = stacked(split_3(near), orders) + stacked(split_3(meet), orders)
        rows += stacked(split_3(rest), orders[:3]) + [blank]
        return jnp.concatenate(rows, axis=0).astype(BF16)

    def prepare_receiving(number, block):
        moved, scaled, norm, inner, density, pressure, mass = fields(block)
        near = jnp.where(row_8 < 3, scaled, by_row(0.0, 0.0, 0.0, norm, 1.0, 0.0))
        meet = jnp.concatenate([moved[3:6], moved[0:3], inner, jnp.ones((1, PB), F32)], axis=0)
        sparse = [
            columns_of(near, blank, blank, second_order),
            columns_of(blank, meet, blank, second_order),
            columns_of(blank, blank, by_row(density, 1.0, 0.0), second_order),
            columns_of(blank, blank, by_row(0.0, 0.0, pressure, 1.0, 0.0), second_order),
        ]
        for k in range(4):
            receiving[number, :, k * PB : (k + 1) * PB] = sparse[k]

    def prepare_acting(number, block):
        moved, scaled, norm, inner, density, pressure, mass = fields(block)
        near = jnp.where(row_8 < 3, -2.0 * scaled, by_row(0.0, 0.0, 0.0, 1.0, norm, 0.0))
        meet = jnp.where(row_8 < 6, -moved, jnp.where(row_8 == 6, 1.0, inner)) * mass
        rest = by_row(1.0, density, mass, mass * pressure, 0.0)
        acting[number] = columns_of(near, meet, rest, first_order)
        spot = split_3(jnp.where(row_8 < 3, moved, jnp.where(row_8 == 3, 1.0, 0.0)))
        summing[number, :, 0:PB] = jnp.concatenate([*spot, blank], axis=0).astype(BF16)
        summing[number, :, PB:] = jnp.concatenate([spot[0], spot[1], blank, blank], axis=0).astype(BF16)

    def block_at(ref, number):
        return ref[:, pl.ds(pl.multiple_of(number * PB, PB), PB)]

    def each_receiving(number, carry):
        prepare_receiving(number, block_at(columns[0], number))
        prepare_receiving(number + BLK_DEV, block_at(partner, number))
        return carry

    def each_acting(number, carry):
        for shift in range(shifts):
            prepare_acting(shift * dev_blocks + number, block_at(columns[shift], number))
        return carry

    lax.fori_loop(0, BLK_DEV, each_receiving, 0)
    receiving[2 * BLK_DEV] = jnp.zeros(receiving.shape[1:], BF16)
    lax.fori_loop(0, dev_blocks, each_acting, 0)
    sums[...] = jnp.zeros(sums.shape, F32)
    copy.wait()

    def work(turn, carry):
        items = [codes_smem[0, turn * UNROLL + lot] for lot in range(UNROLL)]
        targets = [lax.shift_right_logical(item, 10) for item in items]
        sources = [item & 1023 for item in items]
        for lot in range(UNROLL):
            products[lot] = lax.dot_general(
                acting[sources[lot]],
                receiving[targets[lot]],
                (((0,), (0,)), ((), ())),
                preferred_element_type=F32,
            )
        closings = []
        for lot in range(UNROLL):
            closing_sum = jnp.zeros((8, PB), F32)
            for start in range(0, PB, ROWS):
                span = slice(start, start + ROWS)
                dist_sq = jnp.maximum(products[lot, span, 0:PB], 1e-12)
                approach = products[lot, span, PB : 2 * PB]
                support = jnp.maximum(KAPPA - dist_sq * lax.rsqrt(dist_sq), 0.0)
                gradient = support * support * support
                closing = approach * gradient
                weight = (dist_sq + 0.01 * SMOOTHING * SMOOTHING * SCALE_SQ) * products[
                    lot, span, 2 * PB : 3 * PB
                ]
                damping = jnp.minimum(approach, 0.0) * pl.reciprocal(weight, approx=True)
                push = (products[lot, span, 3 * PB :] + damping) * gradient
                high = push.astype(BF16)
                parts[lot, start : start + ROWS, :] = high
                parts[lot, PB + start : PB + start + ROWS, :] = (push - high.astype(F32)).astype(BF16)
                for part in range(0, ROWS, 8):
                    closing_sum = closing_sum + closing[part : part + 8]
            closings.append(closing_sum)
        for lot in range(UNROLL):
            total = jnp.dot(summing[sources[lot]], parts[lot], preferred_element_type=F32)
            sums[targets[lot], 0:8, :] += closings[lot]
            sums[targets[lot], 8:16, :] += total[0:8] + total[8:16] + total[16:24]
        return carry

    lax.fori_loop(0, lax.div(count + UNROLL - 1, UNROLL), work, 0)

    for number in range(BLK_DEV):
        place = slice(number * PB, (number + 1) * PB)
        for base, source, out in ((0, columns[0], own_out), (BLK_DEV, partner, other_out)):
            out[0:1, place] = -jnp.sum(sums[base + number, 0:8, :], axis=0, keepdims=True)
            out[1:4, place] = (source[0:3, place] - CENTRE) * sums[base + number, 11:12, :] - sums[
                base + number, 8:11, :
            ]


def finish_kernel(step_index, time_step, particles, own, other, rates_out, advanced_out):
    step_length = time_step[0]
    elapsed = step_index[0].astype(F32) * step_length
    strength = BLAST_STRENGTH * jnp.exp(jnp.full((1, PB), -elapsed / DECAY_TIME, F32))[:, 0:1]
    block = particles[...]
    tile_rates = own[...] + other[...]
    relative = block[0:3] + 1.0
    spread_sq = jnp.sum(relative * relative, axis=0, keepdims=True) + 1.0
    source = strength * relative / (spread_sq * jnp.sqrt(spread_sq))
    forcing = tile_rates[1:4] + source
    rates_out[0:1] = tile_rates[0:1]
    rates_out[1:4] = forcing
    velocity = block[3:6] + step_length * forcing
    advanced_out[0:3] = block[0:3] + step_length * velocity
    advanced_out[3:6] = velocity
    advanced_out[6:7] = block[6:7] + step_length * tile_rates[0:1]


def pair_sums(columns, partner, rim):
    shifts, width = len(columns), partner.shape[1] - PB
    dev_blocks = BLK_DEV + 2 * rim
    receivers, actors = 2 * BLK_DEV + 1, shifts * dev_blocks
    slots = 3 * PB
    partial = jax.ShapeDtypeStruct((4, width), F32)
    return pl.pallas_call(
        functools.partial(pair_kernel, shifts, rim),
        out_shape=(partial, partial),
        in_specs=[VMEM] * (shifts + 1),
        out_specs=(VMEM, VMEM),
        scratch_shapes=[
            pltpu.VMEM((actors, PB, PB), BF16),
            pltpu.VMEM((actors, 32, 2 * PB), BF16),
            pltpu.VMEM((receivers, PB, 4 * PB), BF16),
            pltpu.VMEM((receivers, 16, PB), F32),
            pltpu.VMEM((UNROLL, PB, 4 * PB), F32),
            pltpu.VMEM((UNROLL, 2 * PB, PB), BF16),
            pltpu.VMEM((3, 2 * shifts, PB), F32),
            pltpu.VMEM((8, slots), jnp.int32),
            pltpu.SMEM((8, slots), jnp.int32),
            pltpu.SemaphoreType.DMA,
        ],
        compiler_params=PARAMS,
        name="pairs",
    )(*columns, partner)


def on_device(
    particles, halo_up, halo_down, tile_first, tile_second, tile_live, step_index, time_step
):
    width = particles.shape[1]
    rim = halo_up.shape[0]
    rim_width = rim * PB
    tiles, slabs = lax.axis_size("tile"), lax.axis_size("slab")
    shifts = tiles // 2
    pair, sent_up, sent_down = pl.pallas_call(
        pre_kernel,
        out_shape=(
            jax.ShapeDtypeStruct((8, width + PB), F32),
            jax.ShapeDtypeStruct((8, rim_width), F32),
            jax.ShapeDtypeStruct((8, rim_width), F32),
        ),
        in_specs=[SMEM, SMEM, VMEM, VMEM, VMEM, VMEM],
        out_specs=(VMEM, VMEM, VMEM),
        name="pack",
    )(halo_up, halo_down, particles, tile_first, tile_second, tile_live)
    across = [(i, i ^ 1) for i in range(tiles)]
    partner = lax.ppermute(pair, "tile", across)
    below = lax.ppermute(sent_up, "slab", [(i, i + 1) for i in range(slabs - 1)])
    above = lax.ppermute(sent_down, "slab", [(i + 1, i) for i in range(slabs - 1)])
    column = pl.pallas_call(
        mid_kernel,
        out_shape=jax.ShapeDtypeStruct((8, width + 2 * rim_width + PB), F32),
        in_specs=[VMEM] * 4,
        out_specs=VMEM,
        name="join",
    )(pair, partner, below, above)
    columns = [column]
    for shift in range(1, shifts):
        ring = [(i, (i + 2 * shift) % tiles) for i in range(tiles)]
        columns.append(lax.ppermute(column, "tile", ring))
    own, other = pair_sums(columns, partner, rim)
    other = lax.ppermute(other, "tile", across)
    return pl.pallas_call(
        finish_kernel,
        out_shape=(
            jax.ShapeDtypeStruct((4, width), F32),
            jax.ShapeDtypeStruct((7, width), F32),
        ),
        in_specs=[SMEM, SMEM, VMEM, VMEM, VMEM],
        out_specs=(VMEM, VMEM),
        name="advance",
    )(step_index, time_step, particles, own, other)


def solution(mesh):
    placed = (
        P(None, ("slab", "tile")),
        P(("slab", "tile")),
        P(("slab", "tile")),
        P("slab", "tile"),
        P("slab", "tile"),
        P("slab", "tile"),
        P(),
        P(),
    )
    return jax.shard_map(
        on_device,
        mesh=mesh,
        in_specs=placed,
        out_specs=(P(None, ("slab", "tile")), P(None, ("slab", "tile"))),
        check_vma=False,
    )
```

```python
import functools

import jax
import jax.numpy as jnp
from jax import lax
from jax.experimental import pallas as pl
from jax.experimental.pallas import tpu as pltpu
from jax.sharding import PartitionSpec as P

PB = 128
BLK_DEV = 16

SMOOTHING = 1.0
KERNEL_NORM = 21.0 / (16.0 * 3.141592653589793)
SOUND_SPEED = 10.0
STIFFNESS = SOUND_SPEED * SOUND_SPEED / 7.0
VISCOSITY = 0.1
BLAST_STRENGTH = 8.0
DECAY_TIME = 8.0

KAPPA = (5.0 * KERNEL_NORM) ** (1.0 / 3.0)
SCALE = 0.5 * KAPPA
SCALE_SQ = SCALE * SCALE
CENTRE = 1.5
DENSITY_SCALE = -0.5 / (VISCOSITY * SOUND_SPEED * SMOOTHING * SCALE_SQ)
UNROLL = 8
ROWS = 32

F32 = jnp.float32
BF16 = jnp.bfloat16
VMEM = pl.BlockSpec(memory_space=pltpu.VMEM)
SMEM = pl.BlockSpec(memory_space=pltpu.SMEM)
HBM = pl.BlockSpec(memory_space=pltpu.HBM)
PAIRS = pltpu.CompilerParams(vmem_limit_bytes=48 * 1024 * 1024)
SMALL = pltpu.CompilerParams(vmem_limit_bytes=4 * 1024 * 1024)


def split_3(value):
    first = value.astype(BF16).astype(F32)
    rest = value - first
    second = rest.astype(BF16).astype(F32)
    return first, second, rest - second


def stacked(parts, order):
    return [parts[k] for k in order]


def divided(value, by):
    if by & (by - 1) == 0:
        return lax.shift_right_logical(value, by.bit_length() - 1)
    return jnp.floor((value.astype(F32) + 0.5) * (1.0 / by)).astype(jnp.int32)


def pack_kernel(particles, first, second, live, pair_out, lists, sems):
    width = particles.shape[1]
    moves = [(values, lists.at[kind]) for kind, values in enumerate((first, second, live))]
    moves.append((particles, pair_out.at[:, 0:width]))
    copies = [pltpu.make_async_copy(*move, sems.at[k]) for k, move in enumerate(moves)]
    for copy in copies:
        copy.start()
    for copy in copies:
        copy.wait()
    pair_out[:, width : width + PB] = jnp.zeros((8, PB), F32)
    for kind in range(3):
        pair_out[kind : kind + 1, width : width + PB] = lists[kind].astype(F32)


def rim_kernel(up_ids, down_ids, pair, near_out, far_out):
    is_odd = lax.rem(lax.axis_index("slab"), 2)
    for item in range(up_ids.shape[0]):
        up, down = up_ids[item], down_ids[item]
        change = is_odd * (down - up)
        for number, out in ((up + change, near_out), (down - change, far_out)):
            start = pl.multiple_of(number * PB, PB)
            out[:, item * PB : (item + 1) * PB] = pair[:, pl.ds(start, PB)]


def join_kernel(pair, partner, near, far, column_out):
    width = pair.shape[1] - PB
    rim = near.shape[1]
    slab = lax.axis_index("slab")
    is_odd = lax.rem(slab, 2) == 1
    below = jnp.where(is_odd, near[...], far[...])
    above = jnp.where(is_odd, far[...], near[...])
    column_out[:, 0:width] = pair[:, 0:width]
    column_out[:, width : width + rim] = jnp.where(slab > 0, below, 0.0)
    column_out[:, width + rim : width + 2 * rim] = jnp.where(slab < lax.axis_size("slab") - 1, above, 0.0)
    column_out[:, width + 2 * rim :] = pair[:, width:]
    column_out[3:6, width + 2 * rim :] = partner[0:3, width:]


def pressure_term(density):
    term = STIFFNESS * (density**7 - 1.0) / (density * density)
    return jnp.where(density > 0.0, term, 0.0)


def pair_kernel(shifts, rim, *refs):
    columns = refs[:shifts]
    partner, own_out, other_out = refs[shifts : shifts + 3]
    acting, summing, receiving, sums, products, parts, lists, codes, codes_smem, sem = refs[shifts + 3 :]
    dev_blocks = BLK_DEV + 2 * rim
    tile = lax.axis_index("tile")
    row, column = lax.div(tile, 2), lax.rem(tile, 2)
    list_start = dev_blocks * PB
    holders = 2 * shifts
    slots = codes.shape[1]

    for shift in range(shifts):
        for side in range(2):
            for kind in range(3):
                lists[kind, 2 * shift + side : 2 * shift + side + 1, :] = columns[shift][
                    3 * side + kind : 3 * side + kind + 1, list_start : list_start + PB
                ]
    first = lists[0].astype(jnp.int32)
    second = lists[1].astype(jnp.int32)
    slab_blocks = holders * BLK_DEV
    is_rim = second >= slab_blocks
    rim_number = second - slab_blocks
    is_above = rim_number >= holders * rim
    rim_number = jnp.where(is_above, rim_number - holders * rim, rim_number)
    rim_owner = divided(rim_number, rim)
    owner = jnp.where(is_rim, rim_owner, divided(second, BLK_DEV))
    place = jnp.where(
        is_rim,
        BLK_DEV + rim_number - rim_owner * rim + jnp.where(is_above, rim, 0),
        second & (BLK_DEV - 1),
    )
    behind = row - divided(owner, 2)
    behind = jnp.where(behind < 0, behind + shifts, behind)
    target = divided(first, BLK_DEV)
    mine = (lists[2] > 0.5) & (divided(target, 2) == row) & ((owner & 1) == column)
    receiver = (first & (BLK_DEV - 1)) + jnp.where((target & 1) == column, 0, BLK_DEV)
    code = receiver * 1024 + behind * dev_blocks + place
    chosen = jnp.where(mine, 1.0, 0.0)
    lane = lax.broadcasted_iota(jnp.int32, (PB, PB), 1)
    sublane = lax.broadcasted_iota(jnp.int32, (PB, PB), 0)
    earlier = jnp.where(sublane < lane, 1.0, 0.0).astype(BF16)
    rank = jnp.dot(chosen.astype(BF16), earlier, preferred_element_type=F32)
    counts = jnp.sum(chosen, axis=1, keepdims=True)
    offset = jnp.zeros((1, 1), F32)
    offsets = []
    for holder in range(holders):
        offsets.append(offset)
        offset = offset + counts[holder : holder + 1]
    rank = rank + jnp.concatenate(offsets, axis=0)
    count = jnp.max(offset).astype(jnp.int32)
    rank = jnp.where(mine, rank.astype(jnp.int32), -1)
    dummy = 2 * BLK_DEV * 1024
    spread = lax.broadcasted_iota(jnp.int32, (PB, slots), 1)
    rank_t = jnp.transpose(jnp.concatenate([rank, jnp.zeros((PB - holders, PB), jnp.int32)], axis=0))
    code_t = jnp.transpose(
        jnp.concatenate([code - dummy, jnp.zeros((PB - holders, PB), jnp.int32)], axis=0)
    )
    found = jnp.zeros((8, slots), jnp.int32)
    for holder in range(holders):
        placed = jnp.where(
            rank_t[:, holder : holder + 1] == spread, code_t[:, holder : holder + 1], 0
        )
        for start in range(0, PB, 8):
            found = found + placed[start : start + 8]
    codes[...] = jnp.broadcast_to(jnp.sum(found, axis=0, keepdims=True) + dummy, codes.shape)
    copy = pltpu.make_async_copy(codes, codes_smem, sem)
    copy.start()

    row_8 = lax.broadcasted_iota(jnp.int32, (8, PB), 0)
    centre = jnp.where(row_8 < 3, CENTRE, 0.0)
    scale = jnp.where(row_8 < 3, SCALE, 0.0)
    blank = jnp.zeros((8, PB), F32)

    def fields(block):
        moved = block - centre
        scaled = moved * scale
        norm = jnp.sum(scaled * scaled, axis=0, keepdims=True)
        inner = jnp.sum(moved[0:3] * moved[3:6], axis=0, keepdims=True)
        density = block[6:7]
        return moved, scaled, norm, inner, density * DENSITY_SCALE, pressure_term(density), block[7:8]

    def by_row(*rows):
        value = rows[-1]
        for row, other in zip(range(len(rows) - 2, -1, -1), rows[-2::-1]):
            value = jnp.where(row_8 == row, other, value)
        return value

    first_order, second_order = (0, 1, 0, 1, 2, 0), (0, 0, 1, 1, 0, 2)

    def columns_of(near, meet, rest, orders):
        rows = stacked(split_3(near), orders) + stacked(split_3(meet), orders)
        rows += stacked(split_3(rest), orders[:3]) + [blank]
        return jnp.concatenate(rows, axis=0).astype(BF16)

    def prepare_receiving(number, block):
        moved, scaled, norm, inner, density, pressure, mass = fields(block)
        near = jnp.where(row_8 < 3, scaled, by_row(0.0, 0.0, 0.0, norm, 1.0, 0.0))
        meet = jnp.concatenate([moved[3:6], moved[0:3], inner, jnp.ones((1, PB), F32)], axis=0)
        sparse = [
            columns_of(near, blank, blank, second_order),
            columns_of(blank, meet, blank, second_order),
            columns_of(blank, blank, by_row(density, 1.0, 0.0), second_order),
            columns_of(blank, blank, by_row(0.0, 0.0, pressure, 1.0, 0.0), second_order),
        ]
        for k in range(4):
            receiving[number, :, k * PB : (k + 1) * PB] = sparse[k]

    def prepare_acting(number, block):
        moved, scaled, norm, inner, density, pressure, mass = fields(block)
        near = jnp.where(row_8 < 3, -2.0 * scaled, by_row(0.0, 0.0, 0.0, 1.0, norm, 0.0))
        meet = jnp.where(row_8 < 6, -moved, jnp.where(row_8 == 6, 1.0, inner)) * mass
        rest = by_row(1.0, density, mass, mass * pressure, 0.0)
        acting[number] = columns_of(near, meet, rest, first_order)
        spot = split_3(jnp.where(row_8 < 3, moved, jnp.where(row_8 == 3, 1.0, 0.0)))
        summing[number, :, 0:PB] = jnp.concatenate([*spot, blank], axis=0).astype(BF16)
        summing[number, :, PB:] = jnp.concatenate([spot[0], spot[1], blank, blank], axis=0).astype(BF16)

    def block_at(ref, number):
        return ref[:, pl.ds(pl.multiple_of(number * PB, PB), PB)]

    def each_receiving(number, carry):
        prepare_receiving(number, block_at(columns[0], number))
        prepare_receiving(number + BLK_DEV, block_at(partner, number))
        return carry

    def each_acting(number, carry):
        for shift in range(shifts):
            prepare_acting(shift * dev_blocks + number, block_at(columns[shift], number))
        return carry

    lax.fori_loop(0, BLK_DEV, each_receiving, 0)
    receiving[2 * BLK_DEV] = jnp.zeros(receiving.shape[1:], BF16)
    lax.fori_loop(0, dev_blocks, each_acting, 0)
    sums[...] = jnp.zeros(sums.shape, F32)
    copy.wait()

    def work(turn, carry):
        items = [codes_smem[0, turn * UNROLL + lot] for lot in range(UNROLL)]
        targets = [lax.shift_right_logical(item, 10) for item in items]
        sources = [item & 1023 for item in items]
        for lot in range(UNROLL):
            products[lot] = lax.dot_general(
                acting[sources[lot]],
                receiving[targets[lot]],
                (((0,), (0,)), ((), ())),
                preferred_element_type=F32,
            )
        closings = []
        for lot in range(UNROLL):
            closing_sum = jnp.zeros((8, PB), F32)
            for start in range(0, PB, ROWS):
                span = slice(start, start + ROWS)
                dist_sq = jnp.maximum(products[lot, span, 0:PB], 1e-12)
                approach = products[lot, span, PB : 2 * PB]
                support = jnp.maximum(KAPPA - dist_sq * lax.rsqrt(dist_sq), 0.0)
                gradient = support * support * support
                closing = approach * gradient
                weight = (dist_sq + 0.01 * SMOOTHING * SMOOTHING * SCALE_SQ) * products[
                    lot, span, 2 * PB : 3 * PB
                ]
                damping = jnp.minimum(approach, 0.0) * pl.reciprocal(weight, approx=True)
                push = (products[lot, span, 3 * PB :] + damping) * gradient
                high = push.astype(BF16)
                parts[lot, start : start + ROWS, :] = high
                parts[lot, PB + start : PB + start + ROWS, :] = (push - high.astype(F32)).astype(BF16)
                for part in range(0, ROWS, 8):
                    closing_sum = closing_sum + closing[part : part + 8]
            closings.append(closing_sum)
        for lot in range(UNROLL):
            total = jnp.dot(summing[sources[lot]], parts[lot], preferred_element_type=F32)
            sums[targets[lot], 0:8, :] += closings[lot]
            sums[targets[lot], 8:16, :] += total[0:8] + total[8:16] + total[16:24]
        return carry

    lax.fori_loop(0, lax.div(count + UNROLL - 1, UNROLL), work, 0)

    for number in range(BLK_DEV):
        place = slice(number * PB, (number + 1) * PB)
        for base, source, out in ((0, columns[0], own_out), (BLK_DEV, partner, other_out)):
            out[0:1, place] = -jnp.sum(sums[base + number, 0:8, :], axis=0, keepdims=True)
            out[1:4, place] = (source[0:3, place] - CENTRE) * sums[base + number, 11:12, :] - sums[
                base + number, 8:11, :
            ]


def advance_kernel(step, particles, own, other, rates_out, advanced_out):
    step_length = step[0:1]
    elapsed = step[1:2] * step_length
    strength = BLAST_STRENGTH * jnp.exp(-elapsed / DECAY_TIME)
    step_length, strength = step_length[:, 0:1], strength[:, 0:1]
    block = particles[...]
    tile_rates = own[...] + other[...]
    relative = block[0:3] + 1.0
    spread_sq = jnp.sum(relative * relative, axis=0, keepdims=True) + 1.0
    source = strength * relative / (spread_sq * jnp.sqrt(spread_sq))
    forcing = tile_rates[1:4] + source
    rates_out[0:1] = tile_rates[0:1]
    rates_out[1:4] = forcing
    velocity = block[3:6] + step_length * forcing
    advanced_out[0:3] = block[0:3] + step_length * velocity
    advanced_out[3:6] = velocity
    advanced_out[6:7] = block[6:7] + step_length * tile_rates[0:1]


def pair_sums(columns, partner, rim):
    shifts, width = len(columns), partner.shape[1] - PB
    dev_blocks = BLK_DEV + 2 * rim
    receivers, actors = 2 * BLK_DEV + 1, shifts * dev_blocks
    slots = 3 * PB
    partial = jax.ShapeDtypeStruct((4, width), F32)
    return pl.pallas_call(
        functools.partial(pair_kernel, shifts, rim),
        out_shape=(partial, partial),
        in_specs=[VMEM] * (shifts + 1),
        out_specs=(VMEM, VMEM),
        scratch_shapes=[
            pltpu.VMEM((actors, PB, PB), BF16),
            pltpu.VMEM((actors, 32, 2 * PB), BF16),
            pltpu.VMEM((receivers, PB, 4 * PB), BF16),
            pltpu.VMEM((receivers, 16, PB), F32),
            pltpu.VMEM((UNROLL, PB, 4 * PB), F32),
            pltpu.VMEM((UNROLL, 2 * PB, PB), BF16),
            pltpu.VMEM((3, 2 * shifts, PB), F32),
            pltpu.VMEM((8, slots), jnp.int32),
            pltpu.SMEM((8, slots), jnp.int32),
            pltpu.SemaphoreType.DMA,
        ],
        compiler_params=PAIRS,
        name="pairs",
    )(*columns, partner)


def on_device(
    particles, halo_up, halo_down, tile_first, tile_second, tile_live, step_index, time_step
):
    width = particles.shape[1]
    rim = halo_up.shape[0]
    rim_width = rim * PB
    tiles, slabs = lax.axis_size("tile"), lax.axis_size("slab")
    shifts = tiles // 2
    given = (particles, tile_first, tile_second, tile_live)
    given = [pltpu.with_memory_space_constraint(array, pltpu.HBM) for array in given]
    pair = pl.pallas_call(
        pack_kernel,
        out_shape=jax.ShapeDtypeStruct((8, width + PB), F32),
        in_specs=[HBM] * 4,
        out_specs=VMEM,
        scratch_shapes=[
            pltpu.VMEM((3, 1, tile_first.shape[-1]), jnp.int32),
            pltpu.SemaphoreType.DMA((4,)),
        ],
        compiler_params=SMALL,
        name="pack",
    )(*given)
    across = [(i, i ^ 1) for i in range(tiles)]
    evens = [(i, i ^ 1) for i in range(slabs)]
    odds = [(i, (i + 1 if i % 2 else i - 1) % slabs) for i in range(slabs)]
    partner = lax.ppermute(pair, "tile", across)
    near, far = pl.pallas_call(
        rim_kernel,
        out_shape=[jax.ShapeDtypeStruct((8, rim_width), F32)] * 2,
        in_specs=[SMEM, SMEM, VMEM],
        out_specs=(VMEM, VMEM),
        compiler_params=SMALL,
        name="rim",
    )(halo_up, halo_down, pair)
    near = lax.ppermute(near, "slab", evens)
    far = lax.ppermute(far, "slab", odds)
    column = pl.pallas_call(
        join_kernel,
        out_shape=jax.ShapeDtypeStruct((8, width + 2 * rim_width + PB), F32),
        in_specs=[VMEM] * 4,
        out_specs=VMEM,
        compiler_params=SMALL,
        name="join",
    )(pair, partner, near, far)
    columns = [column] * shifts
    for shift in sorted(range(1, shifts), key=lambda k: min(k, shifts - k)):
        ring = [(i, (i + 2 * shift) % tiles) for i in range(tiles)]
        columns[shift] = lax.ppermute(column, "tile", ring)
    own, other = pair_sums(columns, partner, rim)
    step = jnp.concatenate([time_step, step_index.astype(F32)])
    step = jnp.broadcast_to(step[:, None], (2, PB))
    other = lax.ppermute(other, "tile", across)
    return pl.pallas_call(
        advance_kernel,
        out_shape=(
            jax.ShapeDtypeStruct((4, width), F32),
            jax.ShapeDtypeStruct((7, width), F32),
        ),
        in_specs=[VMEM] * 4,
        out_specs=(VMEM, VMEM),
        compiler_params=SMALL,
        name="advance",
    )(step, particles, own, other)


def solution(mesh):
    placed = (
        P(None, ("slab", "tile")),
        P(("slab", "tile")),
        P(("slab", "tile")),
        P("slab", "tile"),
        P("slab", "tile"),
        P("slab", "tile"),
        P(),
        P(),
    )
    return jax.shard_map(
        on_device,
        mesh=mesh,
        in_specs=placed,
        out_specs=(P(None, ("slab", "tile")), P(None, ("slab", "tile"))),
        check_vma=False,
    )
```

```python
import functools

import jax
import jax.numpy as jnp
from jax import lax
from jax.experimental import pallas as pl
from jax.experimental.pallas import tpu as pltpu
from jax.sharding import PartitionSpec as P

PB = 128
BLK_DEV = 16

SMOOTHING = 1.0
KERNEL_NORM = 21.0 / (16.0 * 3.141592653589793)
SOUND_SPEED = 10.0
STIFFNESS = SOUND_SPEED * SOUND_SPEED / 7.0
VISCOSITY = 0.1
BLAST_STRENGTH = 8.0
DECAY_TIME = 8.0

KAPPA = (5.0 * KERNEL_NORM) ** (1.0 / 3.0)
SCALE = 0.5 * KAPPA
SCALE_SQ = SCALE * SCALE
CENTRE = 1.5
DENSITY_SCALE = -0.5 / (VISCOSITY * SOUND_SPEED * SMOOTHING * SCALE_SQ)
BATCH = 16
ROWS = 32

F32 = jnp.float32
BF16 = jnp.bfloat16
VMEM = pl.BlockSpec(memory_space=pltpu.VMEM)
SMEM = pl.BlockSpec(memory_space=pltpu.SMEM)
HBM = pl.BlockSpec(memory_space=pltpu.HBM)
PAIRS = pltpu.CompilerParams(vmem_limit_bytes=32 * 1024 * 1024)
SMALL = pltpu.CompilerParams(vmem_limit_bytes=4 * 1024 * 1024)


def split_3(value):
    first = value.astype(BF16).astype(F32)
    rest = value - first
    second = rest.astype(BF16).astype(F32)
    return first, second, rest - second


def stacked(parts, order):
    return [parts[k] for k in order]


def divided(value, by):
    if by & (by - 1) == 0:
        return lax.shift_right_logical(value, by.bit_length() - 1)
    return jnp.floor((value.astype(F32) + 0.5) * (1.0 / by)).astype(jnp.int32)


def pack_kernel(particles, first, second, live, pair_out, lists, sems):
    width = particles.shape[1]
    moves = [(values, lists.at[kind]) for kind, values in enumerate((first, second, live))]
    moves.append((particles, pair_out.at[:, 0:width]))
    copies = [pltpu.make_async_copy(*move, sems.at[k]) for k, move in enumerate(moves)]
    for copy in copies:
        copy.start()
    for copy in copies:
        copy.wait()
    pair_out[:, width : width + PB] = jnp.zeros((8, PB), F32)
    for kind in range(3):
        pair_out[kind : kind + 1, width : width + PB] = lists[kind].astype(F32)


def rim_kernel(up_ids, down_ids, pair, near_out, far_out):
    is_odd = lax.rem(lax.axis_index("slab"), 2)
    for item in range(up_ids.shape[0]):
        up, down = up_ids[item], down_ids[item]
        change = is_odd * (down - up)
        for number, out in ((up + change, near_out), (down - change, far_out)):
            start = pl.multiple_of(number * PB, PB)
            out[:, item * PB : (item + 1) * PB] = pair[:, pl.ds(start, PB)]


def join_kernel(pair, partner, near, far, column_out):
    width = pair.shape[1] - PB
    rim = near.shape[1]
    slab = lax.axis_index("slab")
    is_odd = lax.rem(slab, 2) == 1
    below = jnp.where(is_odd, near[...], far[...])
    above = jnp.where(is_odd, far[...], near[...])
    column_out[:, 0:width] = pair[:, 0:width]
    column_out[:, width : width + rim] = jnp.where(slab > 0, below, 0.0)
    column_out[:, width + rim : width + 2 * rim] = jnp.where(slab < lax.axis_size("slab") - 1, above, 0.0)
    column_out[:, width + 2 * rim :] = pair[:, width:]
    column_out[3:6, width + 2 * rim :] = partner[0:3, width:]


def pressure_term(density):
    term = STIFFNESS * (density**7 - 1.0) / (density * density)
    return jnp.where(density > 0.0, term, 0.0)


def add_tiles(codes, row, count, acting, summing, receiving, sums, products, parts):
    def work(first, lots):
        items = [codes[row, first + lot] for lot in range(lots)]
        targets = [lax.shift_right_logical(item, 10) for item in items]
        sources = [item & 1023 for item in items]
        for lot in range(lots):
            products[lot] = lax.dot_general(
                acting[sources[lot]],
                receiving[targets[lot]],
                (((0,), (0,)), ((), ())),
                preferred_element_type=F32,
            )
        closings = []
        for lot in range(lots):
            closing_sum = jnp.zeros((8, PB), F32)
            for start in range(0, PB, ROWS):
                span = slice(start, start + ROWS)
                dist_sq = jnp.maximum(products[lot, span, 0:PB], 1e-12)
                approach = products[lot, span, PB : 2 * PB]
                support = jnp.maximum(KAPPA - dist_sq * lax.rsqrt(dist_sq), 0.0)
                gradient = support * support * support
                closing = approach * gradient
                weight = (dist_sq + 0.01 * SMOOTHING * SMOOTHING * SCALE_SQ) * products[
                    lot, span, 2 * PB : 3 * PB
                ]
                damping = jnp.minimum(approach, 0.0) * pl.reciprocal(weight, approx=True)
                push = (products[lot, span, 3 * PB :] + damping) * gradient
                high = push.astype(BF16)
                parts[lot, start : start + ROWS, :] = high
                parts[lot, PB + start : PB + start + ROWS, :] = (push - high.astype(F32)).astype(BF16)
                for part in range(0, ROWS, 8):
                    closing_sum = closing_sum + closing[part : part + 8]
            closings.append(closing_sum)
        for lot in range(lots):
            total = jnp.dot(summing[sources[lot]], parts[lot], preferred_element_type=F32)
            sums[targets[lot], 0:8, :] += closings[lot]
            sums[targets[lot], 8:16, :] += total[0:8] + total[8:16] + total[16:24]

    def full(turn, carry):
        work(turn * BATCH, BATCH)
        return carry

    half = BATCH // 2
    turns = lax.div(count + half - 1, BATCH)
    lax.fori_loop(0, turns, full, 0)

    @pl.when(count > turns * BATCH)
    def _():
        work(turns * BATCH, half)


def write_rates(sums, base, source, out):
    for block in range(BLK_DEV):
        number, place = base + block, slice(block * PB, (block + 1) * PB)
        out[0:1, place] = -jnp.sum(sums[number, 0:8, :], axis=0, keepdims=True)
        out[1:4, place] = (source[0:3, place] - CENTRE) * sums[number, 11:12, :] - sums[number, 8:11, :]


FIRST_ORDER, SECOND_ORDER = (0, 1, 0, 1, 2, 0), (0, 0, 1, 1, 0, 2)


def row_8():
    return lax.broadcasted_iota(jnp.int32, (8, PB), 0)


def fields(block):
    moved = block - jnp.where(row_8() < 3, CENTRE, 0.0)
    scaled = moved * jnp.where(row_8() < 3, SCALE, 0.0)
    norm = jnp.sum(scaled * scaled, axis=0, keepdims=True)
    inner = jnp.sum(moved[0:3] * moved[3:6], axis=0, keepdims=True)
    density = block[6:7]
    return moved, scaled, norm, inner, density * DENSITY_SCALE, pressure_term(density), block[7:8]


def by_row(*rows):
    value = rows[-1]
    for row, other in zip(range(len(rows) - 2, -1, -1), rows[-2::-1]):
        value = jnp.where(row_8() == row, other, value)
    return value


def columns_of(near, meet, rest, orders):
    rows = stacked(split_3(near), orders) + stacked(split_3(meet), orders)
    rows += stacked(split_3(rest), orders[:3]) + [jnp.zeros((8, PB), F32)]
    return jnp.concatenate(rows, axis=0).astype(BF16)


def prepare_receiving(receiving, number, block):
    moved, scaled, norm, inner, density, pressure, mass = fields(block)
    near = jnp.where(row_8() < 3, scaled, by_row(0.0, 0.0, 0.0, norm, 1.0, 0.0))
    blank = jnp.zeros((8, PB), F32)
    meet = jnp.concatenate([moved[3:6], moved[0:3], inner, jnp.ones((1, PB), F32)], axis=0)
    sparse = [
        columns_of(near, blank, blank, SECOND_ORDER),
        columns_of(blank, meet, blank, SECOND_ORDER),
        columns_of(blank, blank, by_row(density, 1.0, 0.0), SECOND_ORDER),
        columns_of(blank, blank, by_row(0.0, 0.0, pressure, 1.0, 0.0), SECOND_ORDER),
    ]
    for k in range(4):
        receiving[number, :, k * PB : (k + 1) * PB] = sparse[k]


def prepare_acting(acting, summing, number, block):
    blank = jnp.zeros((8, PB), F32)
    moved, scaled, norm, inner, density, pressure, mass = fields(block)
    near = jnp.where(row_8() < 3, -2.0 * scaled, by_row(0.0, 0.0, 0.0, 1.0, norm, 0.0))
    meet = jnp.where(row_8() < 6, -moved, jnp.where(row_8() == 6, 1.0, inner)) * mass
    rest = by_row(1.0, density, mass, mass * pressure, 0.0)
    acting[number] = columns_of(near, meet, rest, FIRST_ORDER)
    spot = split_3(jnp.where(row_8() < 3, moved, jnp.where(row_8() == 3, 1.0, 0.0)))
    summing[number, :, 0:PB] = jnp.concatenate([*spot, blank], axis=0).astype(BF16)
    summing[number, :, PB:] = jnp.concatenate([spot[0], spot[1], blank, blank], axis=0).astype(BF16)


def find_tiles(columns, early, rim, lists, codes, is_early, sides):
    shifts = lax.axis_size("tile") // 2
    dev_blocks = BLK_DEV + 2 * rim
    tile = lax.axis_index("tile")
    row, column = lax.div(tile, 2), lax.rem(tile, 2)
    list_start = dev_blocks * PB
    places = list(columns)
    holders = 2 * len(places)
    for position, shift in enumerate(places):
        for side in range(2):
            for kind in range(3):
                lists[kind, 2 * position + side : 2 * position + side + 1, :] = columns[shift][
                    3 * side + kind : 3 * side + kind + 1, list_start : list_start + PB
                ]
    first = lists[0, 0:holders].astype(jnp.int32)
    second = lists[1, 0:holders].astype(jnp.int32)
    slab_blocks = 2 * shifts * BLK_DEV
    is_rim = second >= slab_blocks
    rim_number = second - slab_blocks
    is_above = rim_number >= 2 * shifts * rim
    rim_number = jnp.where(is_above, rim_number - 2 * shifts * rim, rim_number)
    rim_owner = divided(rim_number, rim)
    owner = jnp.where(is_rim, rim_owner, divided(second, BLK_DEV))
    place = jnp.where(
        is_rim,
        BLK_DEV + rim_number - rim_owner * rim + jnp.where(is_above, rim, 0),
        second & (BLK_DEV - 1),
    )
    behind = row - divided(owner, 2)
    behind = jnp.where(behind < 0, behind + shifts, behind)
    arrival = jnp.zeros_like(behind)
    for position, shift in enumerate(places):
        arrival = jnp.where(behind == shift, position, arrival)
    target = divided(first, BLK_DEV)
    mine = (lists[2, 0:holders] > 0.5) & (divided(target, 2) == row) & ((owner & 1) == column)
    from_early = functools.reduce(jnp.logical_or, [behind == shift for shift in early])
    if is_early:
        mine = mine & from_early
    else:
        held_early = lax.broadcasted_iota(jnp.int32, (holders, PB), 0) < 2 * len(early)
        mine = mine & jnp.logical_not(from_early & held_early)
    is_own = (target & 1) == column
    code = ((first & (BLK_DEV - 1)) + jnp.where(is_own, BLK_DEV, 0)) * 1024 + arrival * dev_blocks + place + 1
    chosen = mine if sides == 1 else jnp.concatenate([mine & jnp.logical_not(is_own), mine & is_own], axis=0)
    lane = lax.broadcasted_iota(jnp.int32, (PB, PB), 1)
    sublane = lax.broadcasted_iota(jnp.int32, (PB, PB), 0)
    ones = jnp.where(chosen, 1.0, 0.0)
    before = jnp.where(sublane < lane, 1.0, 0.0).astype(BF16)
    rank = jnp.dot(ones.astype(BF16), before, preferred_element_type=F32)
    counts = jnp.sum(ones, axis=1, keepdims=True)
    slots = codes.shape[1]
    spots = lax.broadcasted_iota(jnp.int32, (slots, PB), 0)
    for side in range(sides):
        found = jnp.zeros((slots, PB), jnp.int32)
        offset = jnp.zeros((1, 1), F32)
        for holder in range(holders):
            line = slice(side * holders + holder, side * holders + holder + 1)
            order = jnp.where(chosen[line], (rank[line] + offset).astype(jnp.int32), -1)
            found = jnp.where(spots == order, code[holder : holder + 1], found)
            offset = offset + counts[line]
        codes[2 + side : 3 + side, :] = jnp.broadcast_to(offset, (1, slots)).astype(jnp.int32)
        row_sum = jnp.ones((8, PB), BF16)
        high, low = (
            lax.dot_general(
                row_sum, part.astype(F32).astype(BF16), (((1,), (1,)), ((), ())), preferred_element_type=F32
            )
            for part in (lax.shift_right_logical(found, 8), found & 255)
        )
        total = high[0:1].astype(jnp.int32) * 256 + low[0:1].astype(jnp.int32)
        codes[side : side + 1, :] = jnp.where(total == 0, 2 * BLK_DEV * 1024, total - 1)


def block_at(ref, number):
    return ref[:, pl.ds(pl.multiple_of(number * PB, PB), PB)]


def prepare_all_acting(acting, summing, columns, dev_blocks):
    def each(number, carry):
        for position, column in enumerate(columns):
            prepare_acting(acting, summing, position * dev_blocks + number, block_at(column, number))
        return carry

    lax.fori_loop(0, dev_blocks, each, 0)


def early_kernel(early, rim, *refs):
    columns = refs[: len(early)]
    partner, receiving, sums, acting, summing, products, parts, lists, codes, codes_smem, sem = refs[len(early) :]
    find_tiles(dict(zip(early, columns)), early, rim, lists, codes, True, 1)
    copy = pltpu.make_async_copy(codes, codes_smem, sem)
    copy.start()

    def each_receiving(number, carry):
        prepare_receiving(receiving, number, block_at(partner, number))
        prepare_receiving(receiving, BLK_DEV + number, block_at(columns[0], number))
        return carry

    lax.fori_loop(0, BLK_DEV, each_receiving, 0)
    receiving[2 * BLK_DEV] = jnp.zeros(receiving.shape[1:], BF16)
    prepare_all_acting(acting, summing, columns, BLK_DEV + 2 * rim)
    sums[...] = jnp.zeros(sums.shape, F32)
    copy.wait()
    add_tiles(codes_smem, 0, codes_smem[2, 0], acting, summing, receiving, sums, products, parts)


def other_kernel(arrivals, early, rim, *refs):
    columns = refs[: len(arrivals)]
    partner, receiving, sums_in, other_out, codes, acting, summing = refs[len(arrivals) : len(arrivals) + 7]
    sums, products, parts, lists, codes_smem, sem = refs[len(arrivals) + 7 :]
    find_tiles(dict(zip(arrivals, columns)), early, rim, lists, codes, False, 2)
    copy = pltpu.make_async_copy(codes, codes_smem, sem)
    copy.start()
    prepare_all_acting(acting, summing, columns, BLK_DEV + 2 * rim)
    sums[...] = sums_in[...]
    copy.wait()
    add_tiles(codes_smem, 0, codes_smem[2, 0], acting, summing, receiving, sums, products, parts)
    write_rates(sums, 0, partner, other_out)


def own_kernel(
    codes, acting, summing, receiving, sums_in, column, own_out, sums, products, parts, codes_smem, sem
):
    copy = pltpu.make_async_copy(codes, codes_smem, sem)
    copy.start()
    sums[...] = sums_in[...]
    copy.wait()
    add_tiles(codes_smem, 1, codes_smem[3, 0], acting, summing, receiving, sums, products, parts)
    write_rates(sums, BLK_DEV, column, own_out)


def advance_kernel(step, particles, own, other, rates_out, advanced_out):
    step_length = step[0:1]
    elapsed = step[1:2] * step_length
    strength = BLAST_STRENGTH * jnp.exp(-elapsed / DECAY_TIME)
    step_length, strength = step_length[:, 0:1], strength[:, 0:1]
    block = particles[...]
    tile_rates = own[...] + other[...]
    relative = block[0:3] + 1.0
    spread_sq = jnp.sum(relative * relative, axis=0, keepdims=True) + 1.0
    source = strength * relative / (spread_sq * jnp.sqrt(spread_sq))
    forcing = tile_rates[1:4] + source
    rates_out[0:1] = tile_rates[0:1]
    rates_out[1:4] = forcing
    velocity = block[3:6] + step_length * forcing
    advanced_out[0:3] = block[0:3] + step_length * velocity
    advanced_out[3:6] = velocity
    advanced_out[6:7] = block[6:7] + step_length * tile_rates[0:1]


def pair_sums(arrivals, columns, partner, rim):
    width = partner.shape[1] - PB
    dev_blocks = BLK_DEV + 2 * rim
    early = arrivals[:2]
    partial = jax.ShapeDtypeStruct((4, width), F32)
    receiving = jax.ShapeDtypeStruct((2 * BLK_DEV + 1, PB, 4 * PB), BF16)
    sums = jax.ShapeDtypeStruct((2 * BLK_DEV + 1, 16, PB), F32)
    batch_scratch = [pltpu.VMEM((BATCH, PB, 4 * PB), F32), pltpu.VMEM((BATCH, 2 * PB, PB), BF16)]

    def actors(shifts):
        count = len(shifts) * dev_blocks
        return (count, PB, PB), (count, 32, 2 * PB)

    def tables(shifts, slots):
        code = (8, slots)
        return pltpu.VMEM((3, 2 * len(shifts), PB), F32), pltpu.SMEM(code, jnp.int32), pltpu.SemaphoreType.DMA

    lists, codes_smem, sem = tables(early, 2 * PB)
    receiving, sums = pl.pallas_call(
        functools.partial(early_kernel, early, rim),
        out_shape=(receiving, sums),
        in_specs=[VMEM] * (len(early) + 1),
        out_specs=[VMEM] * 2,
        scratch_shapes=[
            *(pltpu.VMEM(shape, BF16) for shape in actors(early)),
            *batch_scratch,
            lists,
            pltpu.VMEM((8, 2 * PB), jnp.int32),
            codes_smem,
            sem,
        ],
        compiler_params=PAIRS,
        cost_estimate=pl.CostEstimate(flops=8_000_000, bytes_accessed=8_000_000, transcendentals=0),
        name="pairs_early",
    )(*(columns[shift] for shift in early), partner)
    lists, codes_smem, sem = tables(arrivals, PB)
    other, *prepared = pl.pallas_call(
        functools.partial(other_kernel, arrivals, early, rim),
        out_shape=(
            partial,
            jax.ShapeDtypeStruct((8, PB), jnp.int32),
            *(jax.ShapeDtypeStruct(shape, BF16) for shape in actors(arrivals)),
        ),
        in_specs=[VMEM] * (len(arrivals) + 3),
        out_specs=[VMEM] * 4,
        scratch_shapes=[pltpu.VMEM(sums.shape, F32), *batch_scratch, lists, codes_smem, sem],
        compiler_params=PAIRS,
        name="pairs_other",
    )(*(columns[shift] for shift in arrivals), partner, receiving, sums)

    def own():
        return pl.pallas_call(
            own_kernel,
            out_shape=partial,
            in_specs=[VMEM] * 6,
            out_specs=VMEM,
            scratch_shapes=[pltpu.VMEM(sums.shape, F32), *batch_scratch, codes_smem, sem],
            compiler_params=PAIRS,
            name="pairs_own",
        )(*prepared, receiving, sums, columns[0])

    return other, own


def on_device(
    particles, halo_up, halo_down, tile_first, tile_second, tile_live, step_index, time_step
):
    width = particles.shape[1]
    rim = halo_up.shape[0]
    rim_width = rim * PB
    tiles, slabs = lax.axis_size("tile"), lax.axis_size("slab")
    shifts = tiles // 2
    given = (particles, tile_first, tile_second, tile_live)
    given = [pltpu.with_memory_space_constraint(array, pltpu.HBM) for array in given]
    pair = pl.pallas_call(
        pack_kernel,
        out_shape=jax.ShapeDtypeStruct((8, width + PB), F32),
        in_specs=[HBM] * 4,
        out_specs=VMEM,
        scratch_shapes=[
            pltpu.VMEM((3, 1, tile_first.shape[-1]), jnp.int32),
            pltpu.SemaphoreType.DMA((4,)),
        ],
        compiler_params=SMALL,
        name="pack",
    )(*given)
    across = [(i, i ^ 1) for i in range(tiles)]
    evens = [(i, i ^ 1) for i in range(slabs)]
    odds = [(i, (i + 1 if i % 2 else i - 1) % slabs) for i in range(slabs)]
    partner = lax.ppermute(pair, "tile", across)
    near, far = pl.pallas_call(
        rim_kernel,
        out_shape=[jax.ShapeDtypeStruct((8, rim_width), F32)] * 2,
        in_specs=[SMEM, SMEM, VMEM],
        out_specs=(VMEM, VMEM),
        compiler_params=SMALL,
        name="rim",
    )(halo_up, halo_down, pair)
    near = lax.ppermute(near, "slab", evens)
    far = lax.ppermute(far, "slab", odds)
    column = pl.pallas_call(
        join_kernel,
        out_shape=jax.ShapeDtypeStruct((8, width + 2 * rim_width + PB), F32),
        in_specs=[VMEM] * 4,
        out_specs=VMEM,
        compiler_params=SMALL,
        name="join",
    )(pair, partner, near, far)
    columns = [column] * shifts
    arrivals = tuple(range(shifts))
    for shift in arrivals[1:]:
        ring = [(i, (i + 2 * shift) % tiles) for i in range(tiles)]
        columns[shift] = lax.ppermute(column, "tile", ring)
    other, own = pair_sums(arrivals, columns, partner, rim)
    step = jnp.concatenate([time_step, step_index.astype(F32)])
    step = jnp.broadcast_to(step[:, None], (2, PB))
    other = lax.ppermute(other, "tile", across)
    return pl.pallas_call(
        advance_kernel,
        out_shape=(
            jax.ShapeDtypeStruct((4, width), F32),
            jax.ShapeDtypeStruct((7, width), F32),
        ),
        in_specs=[VMEM] * 4,
        out_specs=(VMEM, VMEM),
        compiler_params=SMALL,
        name="advance",
    )(step, particles, own(), other)


def solution(mesh):
    placed = (
        P(None, ("slab", "tile")),
        P(("slab", "tile")),
        P(("slab", "tile")),
        P("slab", "tile"),
        P("slab", "tile"),
        P("slab", "tile"),
        P(),
        P(),
    )
    return jax.shard_map(
        on_device,
        mesh=mesh,
        in_specs=placed,
        out_specs=(P(None, ("slab", "tile")), P(None, ("slab", "tile"))),
        check_vma=False,
    )
```

```python
import functools

import jax
import jax.numpy as jnp
from jax import lax
from jax.experimental import pallas as pl
from jax.experimental.pallas import tpu as pltpu
from jax.sharding import PartitionSpec as P

PB = 128
BLK_DEV = 16

SMOOTHING = 1.0
KERNEL_NORM = 21.0 / (16.0 * 3.141592653589793)
SOUND_SPEED = 10.0
STIFFNESS = SOUND_SPEED * SOUND_SPEED / 7.0
VISCOSITY = 0.1
BLAST_STRENGTH = 8.0
DECAY_TIME = 8.0

KAPPA = (5.0 * KERNEL_NORM) ** (1.0 / 3.0)
SCALE = 0.5 * KAPPA
SCALE_SQ = SCALE * SCALE
CENTRE = 1.5
DENSITY_SCALE = -0.5 / (VISCOSITY * SOUND_SPEED * SMOOTHING * SCALE_SQ)
BATCH = 16
ROWS = 32

F32 = jnp.float32
BF16 = jnp.bfloat16
VMEM = pl.BlockSpec(memory_space=pltpu.VMEM)
SMEM = pl.BlockSpec(memory_space=pltpu.SMEM)
HBM = pl.BlockSpec(memory_space=pltpu.HBM)
PAIRS = pltpu.CompilerParams(vmem_limit_bytes=32 * 1024 * 1024)
SMALL = pltpu.CompilerParams(vmem_limit_bytes=4 * 1024 * 1024)


def split_3(value):
    first = value.astype(BF16).astype(F32)
    rest = value - first
    second = rest.astype(BF16).astype(F32)
    return first, second, rest - second


def stacked(parts, order):
    return [parts[k] for k in order]


def divided(value, by):
    if by & (by - 1) == 0:
        return lax.shift_right_logical(value, by.bit_length() - 1)
    return jnp.floor((value.astype(F32) + 0.5) * (1.0 / by)).astype(jnp.int32)


def pack_kernel(particles, first, second, live, pair_out, lists, sems):
    width = particles.shape[1]
    moves = [(values, lists.at[kind]) for kind, values in enumerate((first, second, live))]
    moves.append((particles, pair_out.at[:, 0:width]))
    copies = [pltpu.make_async_copy(*move, sems.at[k]) for k, move in enumerate(moves)]
    for copy in copies:
        copy.start()
    for copy in copies:
        copy.wait()
    pair_out[:, width : width + PB] = jnp.zeros((8, PB), F32)
    for kind in range(3):
        pair_out[kind : kind + 1, width : width + PB] = lists[kind].astype(F32)


def rim_kernel(up_ids, down_ids, pair, near_out, far_out):
    is_odd = lax.rem(lax.axis_index("slab"), 2)
    for item in range(up_ids.shape[0]):
        up, down = up_ids[item], down_ids[item]
        change = is_odd * (down - up)
        for number, out in ((up + change, near_out), (down - change, far_out)):
            start = pl.multiple_of(number * PB, PB)
            out[:, item * PB : (item + 1) * PB] = pair[:, pl.ds(start, PB)]


def join_kernel(pair, partner, far, near, column_out):
    width = pair.shape[1] - PB
    rim = near.shape[1]
    slab = lax.axis_index("slab")
    is_odd = lax.rem(slab, 2) == 1
    below = jnp.where(is_odd, near[...], far[...])
    above = jnp.where(is_odd, far[...], near[...])
    column_out[:, 0:width] = pair[:, 0:width]
    column_out[:, width : width + rim] = jnp.where(slab > 0, below, 0.0)
    column_out[:, width + rim : width + 2 * rim] = jnp.where(slab < lax.axis_size("slab") - 1, above, 0.0)
    column_out[:, width + 2 * rim :] = pair[:, width:]
    column_out[3:6, width + 2 * rim :] = partner[0:3, width:]


def pressure_term(density):
    term = STIFFNESS * (density**7 - 1.0) / (density * density)
    return jnp.where(density > 0.0, term, 0.0)


def add_tiles(codes, row, count, acting, summing, receiving, sums, products, parts):
    def work(first, lots):
        items = [codes[row, first + lot] for lot in range(lots)]
        targets = [lax.shift_right_logical(item, 10) for item in items]
        sources = [item & 1023 for item in items]
        for lot in range(lots):
            products[lot] = lax.dot_general(
                acting[sources[lot]],
                receiving[targets[lot]],
                (((0,), (0,)), ((), ())),
                preferred_element_type=F32,
            )
        closings = []
        for lot in range(lots):
            closing_sum = jnp.zeros((8, PB), F32)
            for start in range(0, PB, ROWS):
                span = slice(start, start + ROWS)
                dist_sq = jnp.maximum(products[lot, span, 0:PB], 1e-12)
                approach = products[lot, span, PB : 2 * PB]
                support = jnp.maximum(KAPPA - dist_sq * lax.rsqrt(dist_sq), 0.0)
                gradient = support * support * support
                closing = approach * gradient
                weight = (dist_sq + 0.01 * SMOOTHING * SMOOTHING * SCALE_SQ) * products[
                    lot, span, 2 * PB : 3 * PB
                ]
                damping = jnp.minimum(approach, 0.0) * pl.reciprocal(weight, approx=True)
                push = (products[lot, span, 3 * PB :] + damping) * gradient
                high = push.astype(BF16)
                parts[lot, start : start + ROWS, :] = high
                parts[lot, PB + start : PB + start + ROWS, :] = (push - high.astype(F32)).astype(BF16)
                for part in range(0, ROWS, 8):
                    closing_sum = closing_sum + closing[part : part + 8]
            closings.append(closing_sum)
        for lot in range(lots):
            total = jnp.dot(summing[sources[lot]], parts[lot], preferred_element_type=F32)
            sums[targets[lot], 0:8, :] += closings[lot]
            sums[targets[lot], 8:16, :] += total[0:8] + total[8:16] + total[16:24]

    def full(turn, carry):
        work(turn * BATCH, BATCH)
        return carry

    half = BATCH // 2
    turns = lax.div(count + half - 1, BATCH)
    lax.fori_loop(0, turns, full, 0)

    @pl.when(count > turns * BATCH)
    def _():
        work(turns * BATCH, half)


def write_rates(sums, base, source, out):
    for block in range(BLK_DEV):
        number, place = base + block, slice(block * PB, (block + 1) * PB)
        out[0:1, place] = -jnp.sum(sums[number, 0:8, :], axis=0, keepdims=True)
        out[1:4, place] = (source[0:3, place] - CENTRE) * sums[number, 11:12, :] - sums[number, 8:11, :]


FIRST_ORDER, SECOND_ORDER = (0, 1, 0, 1, 2, 0), (0, 0, 1, 1, 0, 2)


def row_8():
    return lax.broadcasted_iota(jnp.int32, (8, PB), 0)


def fields(block):
    moved = block - jnp.where(row_8() < 3, CENTRE, 0.0)
    scaled = moved * jnp.where(row_8() < 3, SCALE, 0.0)
    norm = jnp.sum(scaled * scaled, axis=0, keepdims=True)
    inner = jnp.sum(moved[0:3] * moved[3:6], axis=0, keepdims=True)
    density = block[6:7]
    return moved, scaled, norm, inner, density * DENSITY_SCALE, pressure_term(density), block[7:8]


def by_row(*rows):
    value = rows[-1]
    for row, other in zip(range(len(rows) - 2, -1, -1), rows[-2::-1]):
        value = jnp.where(row_8() == row, other, value)
    return value


def columns_of(near, meet, rest, orders):
    rows = stacked(split_3(near), orders) + stacked(split_3(meet), orders)
    rows += stacked(split_3(rest), orders[:3]) + [jnp.zeros((8, PB), F32)]
    return jnp.concatenate(rows, axis=0).astype(BF16)


def prepare_receiving(receiving, number, block):
    moved, scaled, norm, inner, density, pressure, mass = fields(block)
    near = jnp.where(row_8() < 3, scaled, by_row(0.0, 0.0, 0.0, norm, 1.0, 0.0))
    blank = jnp.zeros((8, PB), F32)
    meet = jnp.concatenate([moved[3:6], moved[0:3], inner, jnp.ones((1, PB), F32)], axis=0)
    sparse = [
        columns_of(near, blank, blank, SECOND_ORDER),
        columns_of(blank, meet, blank, SECOND_ORDER),
        columns_of(blank, blank, by_row(density, 1.0, 0.0), SECOND_ORDER),
        columns_of(blank, blank, by_row(0.0, 0.0, pressure, 1.0, 0.0), SECOND_ORDER),
    ]
    for k in range(4):
        receiving[number, :, k * PB : (k + 1) * PB] = sparse[k]


def prepare_acting(acting, summing, number, block):
    blank = jnp.zeros((8, PB), F32)
    moved, scaled, norm, inner, density, pressure, mass = fields(block)
    near = jnp.where(row_8() < 3, -2.0 * scaled, by_row(0.0, 0.0, 0.0, 1.0, norm, 0.0))
    meet = jnp.where(row_8() < 6, -moved, jnp.where(row_8() == 6, 1.0, inner)) * mass
    rest = by_row(1.0, density, mass, mass * pressure, 0.0)
    acting[number] = columns_of(near, meet, rest, FIRST_ORDER)
    spot = split_3(jnp.where(row_8() < 3, moved, jnp.where(row_8() == 3, 1.0, 0.0)))
    summing[number, :, 0:PB] = jnp.concatenate([*spot, blank], axis=0).astype(BF16)
    summing[number, :, PB:] = jnp.concatenate([spot[0], spot[1], blank, blank], axis=0).astype(BF16)


def find_tiles(columns, early, rim, lists, codes, is_early, sides):
    shifts = lax.axis_size("tile") // 2
    dev_blocks = BLK_DEV + 2 * rim
    tile = lax.axis_index("tile")
    row, column = lax.div(tile, 2), lax.rem(tile, 2)
    list_start = dev_blocks * PB
    places = list(columns)
    holders = 2 * len(places)
    for position, shift in enumerate(places):
        for side in range(2):
            for kind in range(3):
                lists[kind, 2 * position + side : 2 * position + side + 1, :] = columns[shift][
                    3 * side + kind : 3 * side + kind + 1, list_start : list_start + PB
                ]
    first = lists[0, 0:holders].astype(jnp.int32)
    second = lists[1, 0:holders].astype(jnp.int32)
    slab_blocks = 2 * shifts * BLK_DEV
    is_rim = second >= slab_blocks
    rim_number = second - slab_blocks
    is_above = rim_number >= 2 * shifts * rim
    rim_number = jnp.where(is_above, rim_number - 2 * shifts * rim, rim_number)
    rim_owner = divided(rim_number, rim)
    owner = jnp.where(is_rim, rim_owner, divided(second, BLK_DEV))
    place = jnp.where(
        is_rim,
        BLK_DEV + rim_number - rim_owner * rim + jnp.where(is_above, rim, 0),
        second & (BLK_DEV - 1),
    )
    behind = row - divided(owner, 2)
    behind = jnp.where(behind < 0, behind + shifts, behind)
    arrival = jnp.zeros_like(behind)
    for position, shift in enumerate(places):
        arrival = jnp.where(behind == shift, position, arrival)
    target = divided(first, BLK_DEV)
    mine = (lists[2, 0:holders] > 0.5) & (divided(target, 2) == row) & ((owner & 1) == column)
    from_early = functools.reduce(jnp.logical_or, [behind == shift for shift in early])
    if is_early:
        mine = mine & from_early
    else:
        held_early = lax.broadcasted_iota(jnp.int32, (holders, PB), 0) < 2 * len(early)
        mine = mine & jnp.logical_not(from_early & held_early)
    is_own = (target & 1) == column
    code = ((first & (BLK_DEV - 1)) + jnp.where(is_own, BLK_DEV, 0)) * 1024 + arrival * dev_blocks + place + 1
    chosen = mine if sides == 1 else jnp.concatenate([mine & jnp.logical_not(is_own), mine & is_own], axis=0)
    lane = lax.broadcasted_iota(jnp.int32, (PB, PB), 1)
    sublane = lax.broadcasted_iota(jnp.int32, (PB, PB), 0)
    ones = jnp.where(chosen, 1.0, 0.0)
    before = jnp.where(sublane < lane, 1.0, 0.0).astype(BF16)
    rank = jnp.dot(ones.astype(BF16), before, preferred_element_type=F32)
    counts = jnp.sum(ones, axis=1, keepdims=True)
    slots = codes.shape[1]
    spots = lax.broadcasted_iota(jnp.int32, (slots, PB), 0)
    for side in range(sides):
        found = jnp.zeros((slots, PB), jnp.int32)
        offset = jnp.zeros((1, 1), F32)
        for holder in range(holders):
            line = slice(side * holders + holder, side * holders + holder + 1)
            order = jnp.where(chosen[line], (rank[line] + offset).astype(jnp.int32), -1)
            found = jnp.where(spots == order, code[holder : holder + 1], found)
            offset = offset + counts[line]
        codes[2 + side : 3 + side, :] = jnp.broadcast_to(offset, (1, slots)).astype(jnp.int32)
        row_sum = jnp.ones((8, PB), BF16)
        high, low = (
            lax.dot_general(
                row_sum, part.astype(F32).astype(BF16), (((1,), (1,)), ((), ())), preferred_element_type=F32
            )
            for part in (lax.shift_right_logical(found, 8), found & 255)
        )
        total = high[0:1].astype(jnp.int32) * 256 + low[0:1].astype(jnp.int32)
        codes[side : side + 1, :] = jnp.where(total == 0, 2 * BLK_DEV * 1024, total - 1)


def block_at(ref, number):
    return ref[:, pl.ds(pl.multiple_of(number * PB, PB), PB)]


def prepare_all_acting(acting, summing, columns, dev_blocks):
    def each(number, carry):
        for position, column in enumerate(columns):
            prepare_acting(acting, summing, position * dev_blocks + number, block_at(column, number))
        return carry

    lax.fori_loop(0, dev_blocks, each, 0)


def early_kernel(early, rim, *refs):
    columns = refs[: len(early)]
    partner, receiving, sums, acting, summing, products, parts, lists, codes, codes_smem, sem = refs[len(early) :]
    find_tiles(dict(zip(early, columns)), early, rim, lists, codes, True, 1)
    copy = pltpu.make_async_copy(codes, codes_smem, sem)
    copy.start()

    def each_receiving(number, carry):
        prepare_receiving(receiving, number, block_at(partner, number))
        prepare_receiving(receiving, BLK_DEV + number, block_at(columns[0], number))
        return carry

    lax.fori_loop(0, BLK_DEV, each_receiving, 0)
    receiving[2 * BLK_DEV] = jnp.zeros(receiving.shape[1:], BF16)
    prepare_all_acting(acting, summing, columns, BLK_DEV + 2 * rim)
    sums[...] = jnp.zeros(sums.shape, F32)
    copy.wait()
    add_tiles(codes_smem, 0, codes_smem[2, 0], acting, summing, receiving, sums, products, parts)


def other_kernel(arrivals, early, rim, *refs):
    columns = refs[: len(arrivals)]
    partner, receiving, sums_in, other_out, codes, acting, summing = refs[len(arrivals) : len(arrivals) + 7]
    sums, products, parts, lists, codes_smem, sem = refs[len(arrivals) + 7 :]
    find_tiles(dict(zip(arrivals, columns)), early, rim, lists, codes, False, 2)
    copy = pltpu.make_async_copy(codes, codes_smem, sem)
    copy.start()
    prepare_all_acting(acting, summing, columns, BLK_DEV + 2 * rim)
    sums[...] = sums_in[...]
    copy.wait()
    add_tiles(codes_smem, 0, codes_smem[2, 0], acting, summing, receiving, sums, products, parts)
    write_rates(sums, 0, partner, other_out)


def own_kernel(
    codes, acting, summing, receiving, sums_in, column, own_out, sums, products, parts, codes_smem, sem
):
    copy = pltpu.make_async_copy(codes, codes_smem, sem)
    copy.start()
    sums[...] = sums_in[...]
    copy.wait()
    add_tiles(codes_smem, 1, codes_smem[3, 0], acting, summing, receiving, sums, products, parts)
    write_rates(sums, BLK_DEV, column, own_out)


def advance_kernel(step, particles, own, other, rates_out, advanced_out):
    step_length = step[0:1]
    elapsed = step[1:2] * step_length
    strength = BLAST_STRENGTH * jnp.exp(-elapsed / DECAY_TIME)
    step_length, strength = step_length[:, 0:1], strength[:, 0:1]
    block = particles[...]
    tile_rates = own[...] + other[...]
    relative = block[0:3] + 1.0
    spread_sq = jnp.sum(relative * relative, axis=0, keepdims=True) + 1.0
    source = strength * relative / (spread_sq * jnp.sqrt(spread_sq))
    forcing = tile_rates[1:4] + source
    rates_out[0:1] = tile_rates[0:1]
    rates_out[1:4] = forcing
    velocity = block[3:6] + step_length * forcing
    advanced_out[0:3] = block[0:3] + step_length * velocity
    advanced_out[3:6] = velocity
    advanced_out[6:7] = block[6:7] + step_length * tile_rates[0:1]


def pair_sums(arrivals, columns, partner, rim):
    width = partner.shape[1] - PB
    dev_blocks = BLK_DEV + 2 * rim
    early = arrivals[:2]
    partial = jax.ShapeDtypeStruct((4, width), F32)
    receiving = jax.ShapeDtypeStruct((2 * BLK_DEV + 1, PB, 4 * PB), BF16)
    sums = jax.ShapeDtypeStruct((2 * BLK_DEV + 1, 16, PB), F32)
    batch_scratch = [pltpu.VMEM((BATCH, PB, 4 * PB), F32), pltpu.VMEM((BATCH, 2 * PB, PB), BF16)]

    def actors(shifts):
        count = len(shifts) * dev_blocks
        return (count, PB, PB), (count, 32, 2 * PB)

    def tables(shifts, slots):
        code = (8, slots)
        return pltpu.VMEM((3, 2 * len(shifts), PB), F32), pltpu.SMEM(code, jnp.int32), pltpu.SemaphoreType.DMA

    lists, codes_smem, sem = tables(early, 2 * PB)
    receiving, sums = pl.pallas_call(
        functools.partial(early_kernel, early, rim),
        out_shape=(receiving, sums),
        in_specs=[VMEM] * (len(early) + 1),
        out_specs=[VMEM] * 2,
        scratch_shapes=[
            *(pltpu.VMEM(shape, BF16) for shape in actors(early)),
            *batch_scratch,
            lists,
            pltpu.VMEM((8, 2 * PB), jnp.int32),
            codes_smem,
            sem,
        ],
        compiler_params=PAIRS,
        cost_estimate=pl.CostEstimate(flops=8_000_000, bytes_accessed=8_000_000, transcendentals=0),
        name="pairs_early",
    )(*(columns[shift] for shift in early), partner)
    lists, codes_smem, sem = tables(arrivals, PB)
    other, *prepared = pl.pallas_call(
        functools.partial(other_kernel, arrivals, early, rim),
        out_shape=(
            partial,
            jax.ShapeDtypeStruct((8, PB), jnp.int32),
            *(jax.ShapeDtypeStruct(shape, BF16) for shape in actors(arrivals)),
        ),
        in_specs=[VMEM] * (len(arrivals) + 3),
        out_specs=[VMEM] * 4,
        scratch_shapes=[pltpu.VMEM(sums.shape, F32), *batch_scratch, lists, codes_smem, sem],
        compiler_params=PAIRS,
        name="pairs_other",
    )(*(columns[shift] for shift in arrivals), partner, receiving, sums)

    def own():
        return pl.pallas_call(
            own_kernel,
            out_shape=partial,
            in_specs=[VMEM] * 6,
            out_specs=VMEM,
            scratch_shapes=[pltpu.VMEM(sums.shape, F32), *batch_scratch, codes_smem, sem],
            compiler_params=PAIRS,
            name="pairs_own",
        )(*prepared, receiving, sums, columns[0])

    return other, own


def on_device(
    particles, halo_up, halo_down, tile_first, tile_second, tile_live, step_index, time_step
):
    width = particles.shape[1]
    rim = halo_up.shape[0]
    rim_width = rim * PB
    tiles, slabs = lax.axis_size("tile"), lax.axis_size("slab")
    shifts = tiles // 2
    given = (particles, tile_first, tile_second, tile_live)
    given = [pltpu.with_memory_space_constraint(array, pltpu.HBM) for array in given]
    pair = pl.pallas_call(
        pack_kernel,
        out_shape=jax.ShapeDtypeStruct((8, width + PB), F32),
        in_specs=[HBM] * 4,
        out_specs=VMEM,
        scratch_shapes=[
            pltpu.VMEM((3, 1, tile_first.shape[-1]), jnp.int32),
            pltpu.SemaphoreType.DMA((4,)),
        ],
        compiler_params=SMALL,
        name="pack",
    )(*given)
    across = [(i, i ^ 1) for i in range(tiles)]
    evens = [(i, i ^ 1) for i in range(slabs)]
    odds = [(i, (i + 1 if i % 2 else i - 1) % slabs) for i in range(slabs)]
    partner = lax.ppermute(pair, "tile", across)
    near, far = pl.pallas_call(
        rim_kernel,
        out_shape=[jax.ShapeDtypeStruct((8, rim_width), F32)] * 2,
        in_specs=[SMEM, SMEM, VMEM],
        out_specs=(VMEM, VMEM),
        compiler_params=SMALL,
        name="rim",
    )(halo_up, halo_down, pair)
    far = lax.ppermute(far, "slab", odds)
    near = lax.ppermute(near, "slab", evens)
    column = pl.pallas_call(
        join_kernel,
        out_shape=jax.ShapeDtypeStruct((8, width + 2 * rim_width + PB), F32),
        in_specs=[VMEM] * 4,
        out_specs=VMEM,
        compiler_params=SMALL,
        name="join",
    )(pair, partner, far, near)
    columns = [column] * shifts
    arrivals = tuple(range(shifts))
    for shift in arrivals[1:]:
        ring = [(i, (i + 2 * shift) % tiles) for i in range(tiles)]
        columns[shift] = lax.ppermute(column, "tile", ring)
    other, own = pair_sums(arrivals, columns, partner, rim)
    step = jnp.concatenate([time_step, step_index.astype(F32)])
    step = jnp.broadcast_to(step[:, None], (2, PB))
    other = lax.ppermute(other, "tile", across)
    return pl.pallas_call(
        advance_kernel,
        out_shape=(
            jax.ShapeDtypeStruct((4, width), F32),
            jax.ShapeDtypeStruct((7, width), F32),
        ),
        in_specs=[VMEM] * 4,
        out_specs=(VMEM, VMEM),
        compiler_params=SMALL,
        name="advance",
    )(step, particles, own(), other)


def solution(mesh):
    placed = (
        P(None, ("slab", "tile")),
        P(("slab", "tile")),
        P(("slab", "tile")),
        P("slab", "tile"),
        P("slab", "tile"),
        P("slab", "tile"),
        P(),
        P(),
    )
    return jax.shard_map(
        on_device,
        mesh=mesh,
        in_specs=placed,
        out_specs=(P(None, ("slab", "tile")), P(None, ("slab", "tile"))),
        check_vma=False,
    )
```

```python
import functools

import jax
import jax.numpy as jnp
from jax import lax
from jax.experimental import pallas as pl
from jax.experimental.pallas import tpu as pltpu
from jax.sharding import PartitionSpec as P

PB = 128
BLK_DEV = 16

SMOOTHING = 1.0
KERNEL_NORM = 21.0 / (16.0 * 3.141592653589793)
SOUND_SPEED = 10.0
STIFFNESS = SOUND_SPEED * SOUND_SPEED / 7.0
VISCOSITY = 0.1
BLAST_STRENGTH = 8.0
DECAY_TIME = 8.0

KAPPA = (5.0 * KERNEL_NORM) ** (1.0 / 3.0)
SCALE = 0.5 * KAPPA
SCALE_SQ = SCALE * SCALE
CENTRE = 1.5
DENSITY_SCALE = -0.5 / (VISCOSITY * SOUND_SPEED * SMOOTHING * SCALE_SQ)
BATCH = 32
ROWS = 32

F32 = jnp.float32
BF16 = jnp.bfloat16
VMEM = pl.BlockSpec(memory_space=pltpu.VMEM)
SMEM = pl.BlockSpec(memory_space=pltpu.SMEM)
HBM = pl.BlockSpec(memory_space=pltpu.HBM)
PAIRS = pltpu.CompilerParams(vmem_limit_bytes=32 * 1024 * 1024)
SMALL = pltpu.CompilerParams(vmem_limit_bytes=4 * 1024 * 1024)


def split_3(value):
    first = value.astype(BF16).astype(F32)
    rest = value - first
    second = rest.astype(BF16).astype(F32)
    return first, second, rest - second


def stacked(parts, order):
    return [parts[k] for k in order]


def divided(value, by):
    if by & (by - 1) == 0:
        return lax.shift_right_logical(value, by.bit_length() - 1)
    return jnp.floor((value.astype(F32) + 0.5) * (1.0 / by)).astype(jnp.int32)


def pack_kernel(particles, first, second, live, pair_out, lists, sems):
    width = particles.shape[1]
    moves = [(values, lists.at[kind]) for kind, values in enumerate((first, second, live))]
    moves.append((particles, pair_out.at[:, 0:width]))
    copies = [pltpu.make_async_copy(*move, sems.at[k]) for k, move in enumerate(moves)]
    for copy in copies:
        copy.start()
    for copy in copies:
        copy.wait()
    pair_out[:, width : width + PB] = jnp.zeros((8, PB), F32)
    for kind in range(3):
        pair_out[kind : kind + 1, width : width + PB] = lists[kind].astype(F32)


def rim_kernel(up_ids, down_ids, pair, near_out, far_out):
    is_odd = lax.rem(lax.axis_index("slab"), 2)
    for item in range(up_ids.shape[0]):
        up, down = up_ids[item], down_ids[item]
        change = is_odd * (down - up)
        for number, out in ((up + change, near_out), (down - change, far_out)):
            start = pl.multiple_of(number * PB, PB)
            out[:, item * PB : (item + 1) * PB] = pair[:, pl.ds(start, PB)]


def join_kernel(pair, partner, far, near, column_out):
    width = pair.shape[1] - PB
    rim = near.shape[1]
    slab = lax.axis_index("slab")
    is_odd = lax.rem(slab, 2) == 1
    below = jnp.where(is_odd, near[...], far[...])
    above = jnp.where(is_odd, far[...], near[...])
    column_out[:, 0:width] = pair[:, 0:width]
    column_out[:, width : width + rim] = jnp.where(slab > 0, below, 0.0)
    column_out[:, width + rim : width + 2 * rim] = jnp.where(slab < lax.axis_size("slab") - 1, above, 0.0)
    column_out[:, width + 2 * rim :] = pair[:, width:]
    column_out[3:6, width + 2 * rim :] = partner[0:3, width:]


def pressure_term(density):
    term = STIFFNESS * (density**7 - 1.0) / (density * density)
    return jnp.where(density > 0.0, term, 0.0)


def add_tiles(codes, row, count, acting, summing, receiving, sums, products, parts):
    def work(first, lots):
        items = [codes[row, first + lot] for lot in range(lots)]
        targets = [lax.shift_right_logical(item, 10) for item in items]
        sources = [item & 1023 for item in items]
        for lot in range(lots):
            products[lot] = lax.dot_general(
                acting[sources[lot]],
                receiving[targets[lot]],
                (((0,), (0,)), ((), ())),
                preferred_element_type=F32,
            )
        closings = []
        for lot in range(lots):
            closing_sum = jnp.zeros((8, PB), F32)
            for start in range(0, PB, ROWS):
                span = slice(start, start + ROWS)
                dist_sq = jnp.maximum(products[lot, span, 0:PB], 1e-12)
                approach = products[lot, span, PB : 2 * PB]
                support = jnp.maximum(KAPPA - dist_sq * lax.rsqrt(dist_sq), 0.0)
                gradient = support * support * support
                closing = approach * gradient
                weight = (dist_sq + 0.01 * SMOOTHING * SMOOTHING * SCALE_SQ) * products[
                    lot, span, 2 * PB : 3 * PB
                ]
                damping = jnp.minimum(approach, 0.0) * pl.reciprocal(weight, approx=True)
                push = (products[lot, span, 3 * PB :] + damping) * gradient
                high = push.astype(BF16)
                parts[lot, start : start + ROWS, :] = high
                parts[lot, PB + start : PB + start + ROWS, :] = (push - high.astype(F32)).astype(BF16)
                for part in range(0, ROWS, 8):
                    closing_sum = closing_sum + closing[part : part + 8]
            closings.append(closing_sum)
        for lot in range(lots):
            total = jnp.dot(summing[sources[lot]], parts[lot], preferred_element_type=F32)
            sums[targets[lot], 0:8, :] += closings[lot]
            sums[targets[lot], 8:16, :] += total[0:8] + total[8:16] + total[16:24]

    quarter = BATCH // 4
    turns = lax.div(count + quarter - 1, BATCH)

    def full(turn, carry):
        work(turn * BATCH, BATCH)
        return carry

    lax.fori_loop(0, turns, full, 0)
    done = turns * BATCH

    @pl.when(count > done + quarter)
    def _():
        work(done, 2 * quarter)

    done = done + jnp.where(count > done + quarter, 2 * quarter, 0)

    @pl.when(count > done)
    def _():
        work(done, quarter)


def write_rates(sums, base, source, out):
    for block in range(BLK_DEV):
        number, place = base + block, slice(block * PB, (block + 1) * PB)
        out[0:1, place] = -jnp.sum(sums[number, 0:8, :], axis=0, keepdims=True)
        out[1:4, place] = (source[0:3, place] - CENTRE) * sums[number, 11:12, :] - sums[number, 8:11, :]


FIRST_ORDER, SECOND_ORDER = (0, 1, 0, 1, 2, 0), (0, 0, 1, 1, 0, 2)


def row_8():
    return lax.broadcasted_iota(jnp.int32, (8, PB), 0)


def fields(block):
    moved = block - jnp.where(row_8() < 3, CENTRE, 0.0)
    scaled = moved * jnp.where(row_8() < 3, SCALE, 0.0)
    norm = jnp.sum(scaled * scaled, axis=0, keepdims=True)
    inner = jnp.sum(moved[0:3] * moved[3:6], axis=0, keepdims=True)
    density = block[6:7]
    return moved, scaled, norm, inner, density * DENSITY_SCALE, pressure_term(density), block[7:8]


def by_row(*rows):
    value = rows[-1]
    for row, other in zip(range(len(rows) - 2, -1, -1), rows[-2::-1]):
        value = jnp.where(row_8() == row, other, value)
    return value


def columns_of(near, meet, rest, orders):
    rows = stacked(split_3(near), orders) + stacked(split_3(meet), orders)
    rows += stacked(split_3(rest), orders[:3]) + [jnp.zeros((8, PB), F32)]
    return jnp.concatenate(rows, axis=0).astype(BF16)


def prepare_receiving(receiving, number, block):
    moved, scaled, norm, inner, density, pressure, mass = fields(block)
    near = jnp.where(row_8() < 3, scaled, by_row(0.0, 0.0, 0.0, norm, 1.0, 0.0))
    blank = jnp.zeros((8, PB), F32)
    meet = jnp.concatenate([moved[3:6], moved[0:3], inner, jnp.ones((1, PB), F32)], axis=0)
    sparse = [
        columns_of(near, blank, blank, SECOND_ORDER),
        columns_of(blank, meet, blank, SECOND_ORDER),
        columns_of(blank, blank, by_row(density, 1.0, 0.0), SECOND_ORDER),
        columns_of(blank, blank, by_row(0.0, 0.0, pressure, 1.0, 0.0), SECOND_ORDER),
    ]
    for k in range(4):
        receiving[number, :, k * PB : (k + 1) * PB] = sparse[k]


def prepare_acting(acting, summing, number, block):
    blank = jnp.zeros((8, PB), F32)
    moved, scaled, norm, inner, density, pressure, mass = fields(block)
    near = jnp.where(row_8() < 3, -2.0 * scaled, by_row(0.0, 0.0, 0.0, 1.0, norm, 0.0))
    meet = jnp.where(row_8() < 6, -moved, jnp.where(row_8() == 6, 1.0, inner)) * mass
    rest = by_row(1.0, density, mass, mass * pressure, 0.0)
    acting[number] = columns_of(near, meet, rest, FIRST_ORDER)
    spot = split_3(jnp.where(row_8() < 3, moved, jnp.where(row_8() == 3, 1.0, 0.0)))
    summing[number, :, 0:PB] = jnp.concatenate([*spot, blank], axis=0).astype(BF16)
    summing[number, :, PB:] = jnp.concatenate([spot[0], spot[1], blank, blank], axis=0).astype(BF16)


def find_tiles(columns, early, rim, lists, codes, is_early, sides):
    shifts = lax.axis_size("tile") // 2
    dev_blocks = BLK_DEV + 2 * rim
    tile = lax.axis_index("tile")
    row, column = lax.div(tile, 2), lax.rem(tile, 2)
    list_start = dev_blocks * PB
    places = list(columns)
    holders = 2 * len(places)
    for position, shift in enumerate(places):
        for side in range(2):
            for kind in range(3):
                lists[kind, 2 * position + side : 2 * position + side + 1, :] = columns[shift][
                    3 * side + kind : 3 * side + kind + 1, list_start : list_start + PB
                ]
    first = lists[0, 0:holders].astype(jnp.int32)
    second = lists[1, 0:holders].astype(jnp.int32)
    slab_blocks = 2 * shifts * BLK_DEV
    is_rim = second >= slab_blocks
    rim_number = second - slab_blocks
    is_above = rim_number >= 2 * shifts * rim
    rim_number = jnp.where(is_above, rim_number - 2 * shifts * rim, rim_number)
    rim_owner = divided(rim_number, rim)
    owner = jnp.where(is_rim, rim_owner, divided(second, BLK_DEV))
    place = jnp.where(
        is_rim,
        BLK_DEV + rim_number - rim_owner * rim + jnp.where(is_above, rim, 0),
        second & (BLK_DEV - 1),
    )
    behind = row - divided(owner, 2)
    behind = jnp.where(behind < 0, behind + shifts, behind)
    arrival = jnp.zeros_like(behind)
    for position, shift in enumerate(places):
        arrival = jnp.where(behind == shift, position, arrival)
    target = divided(first, BLK_DEV)
    mine = (lists[2, 0:holders] > 0.5) & (divided(target, 2) == row) & ((owner & 1) == column)
    from_early = functools.reduce(jnp.logical_or, [behind == shift for shift in early])
    if is_early:
        mine = mine & from_early
    else:
        held_early = lax.broadcasted_iota(jnp.int32, (holders, PB), 0) < 2 * len(early)
        mine = mine & jnp.logical_not(from_early & held_early)
    is_own = (target & 1) == column
    code = ((first & (BLK_DEV - 1)) + jnp.where(is_own, BLK_DEV, 0)) * 1024 + arrival * dev_blocks + place + 1
    chosen = mine if sides == 1 else jnp.concatenate([mine & jnp.logical_not(is_own), mine & is_own], axis=0)
    lane = lax.broadcasted_iota(jnp.int32, (PB, PB), 1)
    sublane = lax.broadcasted_iota(jnp.int32, (PB, PB), 0)
    ones = jnp.where(chosen, 1.0, 0.0)
    before = jnp.where(sublane < lane, 1.0, 0.0).astype(BF16)
    rank = jnp.dot(ones.astype(BF16), before, preferred_element_type=F32)
    counts = jnp.sum(ones, axis=1, keepdims=True)
    slots = codes.shape[1]
    spots = lax.broadcasted_iota(jnp.int32, (slots, PB), 0)
    for side in range(sides):
        found = jnp.zeros((slots, PB), jnp.int32)
        offset = jnp.zeros((1, 1), F32)
        for holder in range(holders):
            line = slice(side * holders + holder, side * holders + holder + 1)
            order = jnp.where(chosen[line], (rank[line] + offset).astype(jnp.int32), -1)
            found = jnp.where(spots == order, code[holder : holder + 1], found)
            offset = offset + counts[line]
        codes[2 + side : 3 + side, :] = jnp.broadcast_to(offset, (1, slots)).astype(jnp.int32)
        row_sum = jnp.ones((8, PB), BF16)
        high, low = (
            lax.dot_general(
                row_sum, part.astype(F32).astype(BF16), (((1,), (1,)), ((), ())), preferred_element_type=F32
            )
            for part in (lax.shift_right_logical(found, 8), found & 255)
        )
        total = high[0:1].astype(jnp.int32) * 256 + low[0:1].astype(jnp.int32)
        codes[side : side + 1, :] = jnp.where(total == 0, 2 * BLK_DEV * 1024, total - 1)


def block_at(ref, number):
    return ref[:, pl.ds(pl.multiple_of(number * PB, PB), PB)]


def prepare_all_acting(acting, summing, columns, dev_blocks):
    def each(number, carry):
        for position, column in enumerate(columns):
            prepare_acting(acting, summing, position * dev_blocks + number, block_at(column, number))
        return carry

    lax.fori_loop(0, dev_blocks, each, 0)


def early_kernel(early, rim, *refs):
    columns = refs[: len(early)]
    partner, receiving, sums, acting, summing, products, parts, lists, codes, codes_smem, sem = refs[len(early) :]
    find_tiles(dict(zip(early, columns)), early, rim, lists, codes, True, 1)
    copy = pltpu.make_async_copy(codes, codes_smem, sem)
    copy.start()

    def each_receiving(number, carry):
        prepare_receiving(receiving, number, block_at(partner, number))
        prepare_receiving(receiving, BLK_DEV + number, block_at(columns[0], number))
        return carry

    lax.fori_loop(0, BLK_DEV, each_receiving, 0)
    receiving[2 * BLK_DEV] = jnp.zeros(receiving.shape[1:], BF16)
    prepare_all_acting(acting, summing, columns, BLK_DEV + 2 * rim)
    sums[...] = jnp.zeros(sums.shape, F32)
    copy.wait()
    add_tiles(codes_smem, 0, codes_smem[2, 0], acting, summing, receiving, sums, products, parts)


def other_kernel(arrivals, early, rim, *refs):
    columns = refs[: len(arrivals)]
    partner, receiving, sums_in, other_out, codes, acting, summing = refs[len(arrivals) : len(arrivals) + 7]
    sums, products, parts, lists, codes_smem, sem = refs[len(arrivals) + 7 :]
    find_tiles(dict(zip(arrivals, columns)), early, rim, lists, codes, False, 2)
    copy = pltpu.make_async_copy(codes, codes_smem, sem)
    copy.start()
    prepare_all_acting(acting, summing, columns, BLK_DEV + 2 * rim)
    sums[...] = sums_in[...]
    copy.wait()
    add_tiles(codes_smem, 0, codes_smem[2, 0], acting, summing, receiving, sums, products, parts)
    write_rates(sums, 0, partner, other_out)


def own_kernel(
    codes, acting, summing, receiving, sums_in, column, own_out, sums, products, parts, codes_smem, sem
):
    copy = pltpu.make_async_copy(codes, codes_smem, sem)
    copy.start()
    sums[...] = sums_in[...]
    copy.wait()
    add_tiles(codes_smem, 1, codes_smem[3, 0], acting, summing, receiving, sums, products, parts)
    write_rates(sums, BLK_DEV, column, own_out)


def advance_kernel(step, particles, own, other, rates_out, advanced_out):
    step_length = step[0:1]
    elapsed = step[1:2] * step_length
    strength = BLAST_STRENGTH * jnp.exp(-elapsed / DECAY_TIME)
    step_length, strength = step_length[:, 0:1], strength[:, 0:1]
    block = particles[...]
    tile_rates = own[...] + other[...]
    relative = block[0:3] + 1.0
    spread_sq = jnp.sum(relative * relative, axis=0, keepdims=True) + 1.0
    source = strength * relative / (spread_sq * jnp.sqrt(spread_sq))
    forcing = tile_rates[1:4] + source
    rates_out[0:1] = tile_rates[0:1]
    rates_out[1:4] = forcing
    velocity = block[3:6] + step_length * forcing
    advanced_out[0:3] = block[0:3] + step_length * velocity
    advanced_out[3:6] = velocity
    advanced_out[6:7] = block[6:7] + step_length * tile_rates[0:1]


def pair_sums(arrivals, columns, partner, rim):
    width = partner.shape[1] - PB
    dev_blocks = BLK_DEV + 2 * rim
    early = arrivals[:2]
    partial = jax.ShapeDtypeStruct((4, width), F32)
    receiving = jax.ShapeDtypeStruct((2 * BLK_DEV + 1, PB, 4 * PB), BF16)
    sums = jax.ShapeDtypeStruct((2 * BLK_DEV + 1, 16, PB), F32)
    batch_scratch = [pltpu.VMEM((BATCH, PB, 4 * PB), F32), pltpu.VMEM((BATCH, 2 * PB, PB), BF16)]

    def actors(shifts):
        count = len(shifts) * dev_blocks
        return (count, PB, PB), (count, 32, 2 * PB)

    def tables(shifts, slots):
        code = (8, slots)
        return pltpu.VMEM((3, 2 * len(shifts), PB), F32), pltpu.SMEM(code, jnp.int32), pltpu.SemaphoreType.DMA

    lists, codes_smem, sem = tables(early, 2 * PB)
    receiving, sums = pl.pallas_call(
        functools.partial(early_kernel, early, rim),
        out_shape=(receiving, sums),
        in_specs=[VMEM] * (len(early) + 1),
        out_specs=[VMEM] * 2,
        scratch_shapes=[
            *(pltpu.VMEM(shape, BF16) for shape in actors(early)),
            *batch_scratch,
            lists,
            pltpu.VMEM((8, 2 * PB), jnp.int32),
            codes_smem,
            sem,
        ],
        compiler_params=PAIRS,
        cost_estimate=pl.CostEstimate(flops=8_000_000, bytes_accessed=8_000_000, transcendentals=0),
        name="pairs_early",
    )(*(columns[shift] for shift in early), partner)
    lists, codes_smem, sem = tables(arrivals, PB)
    other, *prepared = pl.pallas_call(
        functools.partial(other_kernel, arrivals, early, rim),
        out_shape=(
            partial,
            jax.ShapeDtypeStruct((8, PB), jnp.int32),
            *(jax.ShapeDtypeStruct(shape, BF16) for shape in actors(arrivals)),
        ),
        in_specs=[VMEM] * (len(arrivals) + 3),
        out_specs=[VMEM] * 4,
        scratch_shapes=[pltpu.VMEM(sums.shape, F32), *batch_scratch, lists, codes_smem, sem],
        compiler_params=PAIRS,
        name="pairs_other",
    )(*(columns[shift] for shift in arrivals), partner, receiving, sums)

    def own():
        return pl.pallas_call(
            own_kernel,
            out_shape=partial,
            in_specs=[VMEM] * 6,
            out_specs=VMEM,
            scratch_shapes=[pltpu.VMEM(sums.shape, F32), *batch_scratch, codes_smem, sem],
            compiler_params=PAIRS,
            name="pairs_own",
        )(*prepared, receiving, sums, columns[0])

    return other, own


def on_device(
    particles, halo_up, halo_down, tile_first, tile_second, tile_live, step_index, time_step
):
    width = particles.shape[1]
    rim = halo_up.shape[0]
    rim_width = rim * PB
    tiles, slabs = lax.axis_size("tile"), lax.axis_size("slab")
    shifts = tiles // 2
    given = (particles, tile_first, tile_second, tile_live)
    given = [pltpu.with_memory_space_constraint(array, pltpu.HBM) for array in given]
    pair = pl.pallas_call(
        pack_kernel,
        out_shape=jax.ShapeDtypeStruct((8, width + PB), F32),
        in_specs=[HBM] * 4,
        out_specs=VMEM,
        scratch_shapes=[
            pltpu.VMEM((3, 1, tile_first.shape[-1]), jnp.int32),
            pltpu.SemaphoreType.DMA((4,)),
        ],
        compiler_params=SMALL,
        name="pack",
    )(*given)
    across = [(i, i ^ 1) for i in range(tiles)]
    evens = [(i, i ^ 1) for i in range(slabs)]
    odds = [(i, (i + 1 if i % 2 else i - 1) % slabs) for i in range(slabs)]
    partner = lax.ppermute(pair, "tile", across)
    near, far = pl.pallas_call(
        rim_kernel,
        out_shape=[jax.ShapeDtypeStruct((8, rim_width), F32)] * 2,
        in_specs=[SMEM, SMEM, VMEM],
        out_specs=(VMEM, VMEM),
        compiler_params=SMALL,
        name="rim",
    )(halo_up, halo_down, pair)
    far = lax.ppermute(far, "slab", odds)
    near = lax.ppermute(near, "slab", evens)
    column = pl.pallas_call(
        join_kernel,
        out_shape=jax.ShapeDtypeStruct((8, width + 2 * rim_width + PB), F32),
        in_specs=[VMEM] * 4,
        out_specs=VMEM,
        compiler_params=SMALL,
        name="join",
    )(pair, partner, far, near)
    columns = [column] * shifts
    arrivals = tuple(range(shifts))
    for shift in arrivals[1:]:
        ring = [(i, (i + 2 * shift) % tiles) for i in range(tiles)]
        columns[shift] = lax.ppermute(column, "tile", ring)
    other, own = pair_sums(arrivals, columns, partner, rim)
    step = jnp.concatenate([time_step, step_index.astype(F32)])
    step = jnp.broadcast_to(step[:, None], (2, PB))
    other = lax.ppermute(other, "tile", across)
    return pl.pallas_call(
        advance_kernel,
        out_shape=(
            jax.ShapeDtypeStruct((4, width), F32),
            jax.ShapeDtypeStruct((7, width), F32),
        ),
        in_specs=[VMEM] * 4,
        out_specs=(VMEM, VMEM),
        compiler_params=SMALL,
        name="advance",
    )(step, particles, own(), other)


def solution(mesh):
    placed = (
        P(None, ("slab", "tile")),
        P(("slab", "tile")),
        P(("slab", "tile")),
        P("slab", "tile"),
        P("slab", "tile"),
        P("slab", "tile"),
        P(),
        P(),
    )
    return jax.shard_map(
        on_device,
        mesh=mesh,
        in_specs=placed,
        out_specs=(P(None, ("slab", "tile")), P(None, ("slab", "tile"))),
        check_vma=False,
    )
```

```python
import functools

import jax
import jax.numpy as jnp
from jax import lax
from jax.experimental import pallas as pl
from jax.experimental.pallas import tpu as pltpu
from jax.sharding import PartitionSpec as P

PB = 128
BLK_DEV = 16

SMOOTHING = 1.0
KERNEL_NORM = 21.0 / (16.0 * 3.141592653589793)
SOUND_SPEED = 10.0
STIFFNESS = SOUND_SPEED * SOUND_SPEED / 7.0
VISCOSITY = 0.1
BLAST_STRENGTH = 8.0
DECAY_TIME = 8.0

KAPPA = (5.0 * KERNEL_NORM) ** (1.0 / 3.0)
SCALE = 0.5 * KAPPA
SCALE_SQ = SCALE * SCALE
CENTRE = 1.5
DENSITY_SCALE = -0.5 / (VISCOSITY * SOUND_SPEED * SMOOTHING * SCALE_SQ)
BATCH = 32
ROWS = 32

F32 = jnp.float32
BF16 = jnp.bfloat16
VMEM = pl.BlockSpec(memory_space=pltpu.VMEM)
SMEM = pl.BlockSpec(memory_space=pltpu.SMEM)
HBM = pl.BlockSpec(memory_space=pltpu.HBM)
PAIRS = pltpu.CompilerParams(vmem_limit_bytes=32 * 1024 * 1024)
SMALL = pltpu.CompilerParams(vmem_limit_bytes=4 * 1024 * 1024)


def split_3(value):
    first = value.astype(BF16).astype(F32)
    rest = value - first
    second = rest.astype(BF16).astype(F32)
    return first, second, rest - second


def stacked(parts, order):
    return [parts[k] for k in order]


def divided(value, by):
    if by & (by - 1) == 0:
        return lax.shift_right_logical(value, by.bit_length() - 1)
    return jnp.floor((value.astype(F32) + 0.5) * (1.0 / by)).astype(jnp.int32)


def pack_kernel(particles, first, second, live, pair_out, lists, sems):
    width = particles.shape[1]
    quarter = width // 4
    moves = [(values, lists.at[kind]) for kind, values in enumerate((first, second, live))]
    for start in range(0, width, quarter):
        span = slice(start, start + quarter)
        moves.append((particles.at[:, span], pair_out.at[:, span]))
    copies = [pltpu.make_async_copy(*move, sems.at[k]) for k, move in enumerate(moves)]
    for copy in copies:
        copy.start()
    pair_out[:, width : width + PB] = jnp.zeros((8, PB), F32)
    for kind in range(3):
        copies[kind].wait()
        pair_out[kind : kind + 1, width : width + PB] = lists[kind].astype(F32)
    for copy in copies[3:]:
        copy.wait()


def rim_kernel(up_ids, down_ids, pair, near_out, far_out):
    is_odd = lax.rem(lax.axis_index("slab"), 2)
    for item in range(up_ids.shape[0]):
        up, down = up_ids[item], down_ids[item]
        change = is_odd * (down - up)
        for number, out in ((up + change, near_out), (down - change, far_out)):
            start = pl.multiple_of(number * PB, PB)
            out[:, item * PB : (item + 1) * PB] = pair[:, pl.ds(start, PB)]


def join_kernel(pair, partner, far, near, column_out):
    width = pair.shape[1] - PB
    rim = near.shape[1]
    slab = lax.axis_index("slab")
    is_odd = lax.rem(slab, 2) == 1
    below = jnp.where(is_odd, near[...], far[...])
    above = jnp.where(is_odd, far[...], near[...])
    column_out[:, 0:width] = pair[:, 0:width]
    column_out[:, width : width + rim] = jnp.where(slab > 0, below, 0.0)
    column_out[:, width + rim : width + 2 * rim] = jnp.where(slab < lax.axis_size("slab") - 1, above, 0.0)
    column_out[:, width + 2 * rim :] = pair[:, width:]
    column_out[3:6, width + 2 * rim :] = partner[0:3, width:]


def pressure_term(density):
    term = STIFFNESS * (density**7 - 1.0) / (density * density)
    return jnp.where(density > 0.0, term, 0.0)


def add_tiles(codes, row, count, acting, summing, receiving, sums, products, parts):
    def work(first, lots):
        items = [codes[row, first + lot] for lot in range(lots)]
        targets = [lax.shift_right_logical(item, 10) for item in items]
        sources = [item & 1023 for item in items]
        for lot in range(lots):
            products[lot] = lax.dot_general(
                acting[sources[lot]],
                receiving[targets[lot]],
                (((0,), (0,)), ((), ())),
                preferred_element_type=F32,
            )
        closings = []
        for lot in range(lots):
            closing_sum = jnp.zeros((8, PB), F32)
            for start in range(0, PB, ROWS):
                span = slice(start, start + ROWS)
                dist_sq = jnp.maximum(products[lot, span, 0:PB], 1e-12)
                approach = products[lot, span, PB : 2 * PB]
                support = jnp.maximum(KAPPA - dist_sq * lax.rsqrt(dist_sq), 0.0)
                gradient = support * support * support
                closing = approach * gradient
                weight = (dist_sq + 0.01 * SMOOTHING * SMOOTHING * SCALE_SQ) * products[
                    lot, span, 2 * PB : 3 * PB
                ]
                damping = jnp.minimum(approach, 0.0) * pl.reciprocal(weight, approx=True)
                push = (products[lot, span, 3 * PB :] + damping) * gradient
                high = push.astype(BF16)
                parts[lot, start : start + ROWS, :] = high
                parts[lot, PB + start : PB + start + ROWS, :] = (push - high.astype(F32)).astype(BF16)
                for part in range(0, ROWS, 8):
                    closing_sum = closing_sum + closing[part : part + 8]
            closings.append(closing_sum)
        for lot in range(lots):
            total = jnp.dot(summing[sources[lot]], parts[lot], preferred_element_type=F32)
            sums[targets[lot], 0:8, :] += closings[lot]
            sums[targets[lot], 8:16, :] += total[0:8] + total[8:16] + total[16:24]

    quarter = BATCH // 4
    turns = lax.div(count + quarter - 1, BATCH)

    def full(turn, carry):
        work(turn * BATCH, BATCH)
        return carry

    lax.fori_loop(0, turns, full, 0)
    done = turns * BATCH

    @pl.when(count > done + quarter)
    def _():
        work(done, 2 * quarter)

    done = done + jnp.where(count > done + quarter, 2 * quarter, 0)

    @pl.when(count > done)
    def _():
        work(done, quarter)


def write_rates(sums, base, source, out):
    for block in range(BLK_DEV):
        number, place = base + block, slice(block * PB, (block + 1) * PB)
        out[0:1, place] = -jnp.sum(sums[number, 0:8, :], axis=0, keepdims=True)
        out[1:4, place] = (source[0:3, place] - CENTRE) * sums[number, 11:12, :] - sums[number, 8:11, :]


FIRST_ORDER, SECOND_ORDER = (0, 1, 0, 1, 2, 0), (0, 0, 1, 1, 0, 2)


def row_8():
    return lax.broadcasted_iota(jnp.int32, (8, PB), 0)


def fields(block):
    moved = block - jnp.where(row_8() < 3, CENTRE, 0.0)
    scaled = moved * jnp.where(row_8() < 3, SCALE, 0.0)
    norm = jnp.sum(scaled * scaled, axis=0, keepdims=True)
    inner = jnp.sum(moved[0:3] * moved[3:6], axis=0, keepdims=True)
    density = block[6:7]
    return moved, scaled, norm, inner, density * DENSITY_SCALE, pressure_term(density), block[7:8]


def by_row(*rows):
    value = rows[-1]
    for row, other in zip(range(len(rows) - 2, -1, -1), rows[-2::-1]):
        value = jnp.where(row_8() == row, other, value)
    return value


def columns_of(near, meet, rest, orders):
    rows = stacked(split_3(near), orders) + stacked(split_3(meet), orders)
    rows += stacked(split_3(rest), orders[:3]) + [jnp.zeros((8, PB), F32)]
    return jnp.concatenate(rows, axis=0).astype(BF16)


def prepare_receiving(receiving, number, block):
    moved, scaled, norm, inner, density, pressure, mass = fields(block)
    near = jnp.where(row_8() < 3, scaled, by_row(0.0, 0.0, 0.0, norm, 1.0, 0.0))
    blank = jnp.zeros((8, PB), F32)
    meet = jnp.concatenate([moved[3:6], moved[0:3], inner, jnp.ones((1, PB), F32)], axis=0)
    sparse = [
        columns_of(near, blank, blank, SECOND_ORDER),
        columns_of(blank, meet, blank, SECOND_ORDER),
        columns_of(blank, blank, by_row(density, 1.0, 0.0), SECOND_ORDER),
        columns_of(blank, blank, by_row(0.0, 0.0, pressure, 1.0, 0.0), SECOND_ORDER),
    ]
    for k in range(4):
        receiving[number, :, k * PB : (k + 1) * PB] = sparse[k]


def prepare_acting(acting, summing, number, block):
    blank = jnp.zeros((8, PB), F32)
    moved, scaled, norm, inner, density, pressure, mass = fields(block)
    near = jnp.where(row_8() < 3, -2.0 * scaled, by_row(0.0, 0.0, 0.0, 1.0, norm, 0.0))
    meet = jnp.where(row_8() < 6, -moved, jnp.where(row_8() == 6, 1.0, inner)) * mass
    rest = by_row(1.0, density, mass, mass * pressure, 0.0)
    acting[number] = columns_of(near, meet, rest, FIRST_ORDER)
    spot = split_3(jnp.where(row_8() < 3, moved, jnp.where(row_8() == 3, 1.0, 0.0)))
    summing[number, :, 0:PB] = jnp.concatenate([*spot, blank], axis=0).astype(BF16)
    summing[number, :, PB:] = jnp.concatenate([spot[0], spot[1], blank, blank], axis=0).astype(BF16)


def find_tiles(columns, early, rim, lists, codes, is_early, sides):
    shifts = lax.axis_size("tile") // 2
    dev_blocks = BLK_DEV + 2 * rim
    tile = lax.axis_index("tile")
    row, column = lax.div(tile, 2), lax.rem(tile, 2)
    list_start = dev_blocks * PB
    places = list(columns)
    holders = 2 * len(places)
    for position, shift in enumerate(places):
        for side in range(2):
            for kind in range(3):
                lists[kind, 2 * position + side : 2 * position + side + 1, :] = columns[shift][
                    3 * side + kind : 3 * side + kind + 1, list_start : list_start + PB
                ]
    first = lists[0, 0:holders].astype(jnp.int32)
    second = lists[1, 0:holders].astype(jnp.int32)
    slab_blocks = 2 * shifts * BLK_DEV
    is_rim = second >= slab_blocks
    rim_number = second - slab_blocks
    is_above = rim_number >= 2 * shifts * rim
    rim_number = jnp.where(is_above, rim_number - 2 * shifts * rim, rim_number)
    rim_owner = divided(rim_number, rim)
    owner = jnp.where(is_rim, rim_owner, divided(second, BLK_DEV))
    place = jnp.where(
        is_rim,
        BLK_DEV + rim_number - rim_owner * rim + jnp.where(is_above, rim, 0),
        second & (BLK_DEV - 1),
    )
    behind = row - divided(owner, 2)
    behind = jnp.where(behind < 0, behind + shifts, behind)
    arrival = jnp.zeros_like(behind)
    for position, shift in enumerate(places):
        arrival = jnp.where(behind == shift, position, arrival)
    target = divided(first, BLK_DEV)
    mine = (lists[2, 0:holders] > 0.5) & (divided(target, 2) == row) & ((owner & 1) == column)
    from_early = functools.reduce(jnp.logical_or, [behind == shift for shift in early])
    if is_early:
        mine = mine & from_early
    else:
        held_early = lax.broadcasted_iota(jnp.int32, (holders, PB), 0) < 2 * len(early)
        mine = mine & jnp.logical_not(from_early & held_early)
    is_own = (target & 1) == column
    code = ((first & (BLK_DEV - 1)) + jnp.where(is_own, BLK_DEV, 0)) * 1024 + arrival * dev_blocks + place + 1
    chosen = mine if sides == 1 else jnp.concatenate([mine & jnp.logical_not(is_own), mine & is_own], axis=0)
    lane = lax.broadcasted_iota(jnp.int32, (PB, PB), 1)
    sublane = lax.broadcasted_iota(jnp.int32, (PB, PB), 0)
    ones = jnp.where(chosen, 1.0, 0.0)
    before = jnp.where(sublane < lane, 1.0, 0.0).astype(BF16)
    rank = jnp.dot(ones.astype(BF16), before, preferred_element_type=F32)
    counts = jnp.sum(ones, axis=1, keepdims=True)
    slots = codes.shape[1]
    spots = lax.broadcasted_iota(jnp.int32, (slots, PB), 0)
    for side in range(sides):
        found = jnp.zeros((slots, PB), jnp.int32)
        offset = jnp.zeros((1, 1), F32)
        for holder in range(holders):
            line = slice(side * holders + holder, side * holders + holder + 1)
            order = jnp.where(chosen[line], (rank[line] + offset).astype(jnp.int32), -1)
            found = jnp.where(spots == order, code[holder : holder + 1], found)
            offset = offset + counts[line]
        codes[2 + side : 3 + side, :] = jnp.broadcast_to(offset, (1, slots)).astype(jnp.int32)
        row_sum = jnp.ones((8, PB), BF16)
        high, low = (
            lax.dot_general(
                row_sum, part.astype(F32).astype(BF16), (((1,), (1,)), ((), ())), preferred_element_type=F32
            )
            for part in (lax.shift_right_logical(found, 8), found & 255)
        )
        total = high[0:1].astype(jnp.int32) * 256 + low[0:1].astype(jnp.int32)
        codes[side : side + 1, :] = jnp.where(total == 0, 2 * BLK_DEV * 1024, total - 1)


def block_at(ref, number):
    return ref[:, pl.ds(pl.multiple_of(number * PB, PB), PB)]


def prepare_all_acting(acting, summing, columns, dev_blocks):
    def each(number, carry):
        for position, column in enumerate(columns):
            prepare_acting(acting, summing, position * dev_blocks + number, block_at(column, number))
        return carry

    lax.fori_loop(0, dev_blocks, each, 0)


def early_kernel(early, rim, *refs):
    columns = refs[: len(early)]
    partner, receiving, sums, acting, summing, products, parts, lists, codes, codes_smem, sem = refs[len(early) :]
    find_tiles(dict(zip(early, columns)), early, rim, lists, codes, True, 1)
    copy = pltpu.make_async_copy(codes, codes_smem, sem)
    copy.start()

    def each_receiving(number, carry):
        prepare_receiving(receiving, number, block_at(partner, number))
        prepare_receiving(receiving, BLK_DEV + number, block_at(columns[0], number))
        return carry

    lax.fori_loop(0, BLK_DEV, each_receiving, 0)
    receiving[2 * BLK_DEV] = jnp.zeros(receiving.shape[1:], BF16)
    prepare_all_acting(acting, summing, columns, BLK_DEV + 2 * rim)
    sums[...] = jnp.zeros(sums.shape, F32)
    copy.wait()
    add_tiles(codes_smem, 0, codes_smem[2, 0], acting, summing, receiving, sums, products, parts)


def other_kernel(arrivals, early, rim, *refs):
    columns = refs[: len(arrivals)]
    partner, receiving, sums_in, other_out, codes, acting, summing = refs[len(arrivals) : len(arrivals) + 7]
    sums, products, parts, lists, codes_smem, sem = refs[len(arrivals) + 7 :]
    find_tiles(dict(zip(arrivals, columns)), early, rim, lists, codes, False, 2)
    copy = pltpu.make_async_copy(codes, codes_smem, sem)
    copy.start()
    prepare_all_acting(acting, summing, columns, BLK_DEV + 2 * rim)
    sums[...] = sums_in[...]
    copy.wait()
    add_tiles(codes_smem, 0, codes_smem[2, 0], acting, summing, receiving, sums, products, parts)
    write_rates(sums, 0, partner, other_out)


def own_kernel(
    codes, acting, summing, receiving, sums_in, column, own_out, sums, products, parts, codes_smem, sem
):
    copy = pltpu.make_async_copy(codes, codes_smem, sem)
    copy.start()
    sums[...] = sums_in[...]
    copy.wait()
    add_tiles(codes_smem, 1, codes_smem[3, 0], acting, summing, receiving, sums, products, parts)
    write_rates(sums, BLK_DEV, column, own_out)


def advance_kernel(step, particles, own, other, rates_out, advanced_out):
    step_length = step[0:1]
    elapsed = step[1:2] * step_length
    strength = BLAST_STRENGTH * jnp.exp(-elapsed / DECAY_TIME)
    step_length, strength = step_length[:, 0:1], strength[:, 0:1]
    block = particles[...]
    tile_rates = own[...] + other[...]
    relative = block[0:3] + 1.0
    spread_sq = jnp.sum(relative * relative, axis=0, keepdims=True) + 1.0
    source = strength * relative / (spread_sq * jnp.sqrt(spread_sq))
    forcing = tile_rates[1:4] + source
    rates_out[0:1] = tile_rates[0:1]
    rates_out[1:4] = forcing
    velocity = block[3:6] + step_length * forcing
    advanced_out[0:3] = block[0:3] + step_length * velocity
    advanced_out[3:6] = velocity
    advanced_out[6:7] = block[6:7] + step_length * tile_rates[0:1]


def pair_sums(arrivals, columns, partner, rim):
    width = partner.shape[1] - PB
    dev_blocks = BLK_DEV + 2 * rim
    early = arrivals[:2]
    partial = jax.ShapeDtypeStruct((4, width), F32)
    receiving = jax.ShapeDtypeStruct((2 * BLK_DEV + 1, PB, 4 * PB), BF16)
    sums = jax.ShapeDtypeStruct((2 * BLK_DEV + 1, 16, PB), F32)
    batch_scratch = [pltpu.VMEM((BATCH, PB, 4 * PB), F32), pltpu.VMEM((BATCH, 2 * PB, PB), BF16)]

    def actors(shifts):
        count = len(shifts) * dev_blocks
        return (count, PB, PB), (count, 32, 2 * PB)

    def tables(shifts, slots):
        code = (8, slots)
        return pltpu.VMEM((3, 2 * len(shifts), PB), F32), pltpu.SMEM(code, jnp.int32), pltpu.SemaphoreType.DMA

    lists, codes_smem, sem = tables(early, 2 * PB)
    receiving, sums = pl.pallas_call(
        functools.partial(early_kernel, early, rim),
        out_shape=(receiving, sums),
        in_specs=[VMEM] * (len(early) + 1),
        out_specs=[VMEM] * 2,
        scratch_shapes=[
            *(pltpu.VMEM(shape, BF16) for shape in actors(early)),
            *batch_scratch,
            lists,
            pltpu.VMEM((8, 2 * PB), jnp.int32),
            codes_smem,
            sem,
        ],
        compiler_params=PAIRS,
        cost_estimate=pl.CostEstimate(flops=8_000_000, bytes_accessed=8_000_000, transcendentals=0),
        name="pairs_early",
    )(*(columns[shift] for shift in early), partner)
    lists, codes_smem, sem = tables(arrivals, PB)
    other, *prepared = pl.pallas_call(
        functools.partial(other_kernel, arrivals, early, rim),
        out_shape=(
            partial,
            jax.ShapeDtypeStruct((8, PB), jnp.int32),
            *(jax.ShapeDtypeStruct(shape, BF16) for shape in actors(arrivals)),
        ),
        in_specs=[VMEM] * (len(arrivals) + 3),
        out_specs=[VMEM] * 4,
        scratch_shapes=[pltpu.VMEM(sums.shape, F32), *batch_scratch, lists, codes_smem, sem],
        compiler_params=PAIRS,
        name="pairs_other",
    )(*(columns[shift] for shift in arrivals), partner, receiving, sums)

    def own():
        return pl.pallas_call(
            own_kernel,
            out_shape=partial,
            in_specs=[VMEM] * 6,
            out_specs=VMEM,
            scratch_shapes=[pltpu.VMEM(sums.shape, F32), *batch_scratch, codes_smem, sem],
            compiler_params=PAIRS,
            name="pairs_own",
        )(*prepared, receiving, sums, columns[0])

    return other, own


def on_device(
    particles, halo_up, halo_down, tile_first, tile_second, tile_live, step_index, time_step
):
    width = particles.shape[1]
    rim = halo_up.shape[0]
    rim_width = rim * PB
    tiles, slabs = lax.axis_size("tile"), lax.axis_size("slab")
    shifts = tiles // 2
    given = (particles, tile_first, tile_second, tile_live)
    given = [pltpu.with_memory_space_constraint(array, pltpu.HBM) for array in given]
    pair = pl.pallas_call(
        pack_kernel,
        out_shape=jax.ShapeDtypeStruct((8, width + PB), F32),
        in_specs=[HBM] * 4,
        out_specs=VMEM,
        scratch_shapes=[
            pltpu.VMEM((3, 1, tile_first.shape[-1]), jnp.int32),
            pltpu.SemaphoreType.DMA((7,)),
        ],
        compiler_params=SMALL,
        name="pack",
    )(*given)
    across = [(i, i ^ 1) for i in range(tiles)]
    evens = [(i, i ^ 1) for i in range(slabs)]
    odds = [(i, (i + 1 if i % 2 else i - 1) % slabs) for i in range(slabs)]
    partner = lax.ppermute(pair, "tile", across)
    near, far = pl.pallas_call(
        rim_kernel,
        out_shape=[jax.ShapeDtypeStruct((8, rim_width), F32)] * 2,
        in_specs=[SMEM, SMEM, VMEM],
        out_specs=(VMEM, VMEM),
        compiler_params=SMALL,
        name="rim",
    )(halo_up, halo_down, pair)
    far = lax.ppermute(far, "slab", odds)
    near = lax.ppermute(near, "slab", evens)
    column = pl.pallas_call(
        join_kernel,
        out_shape=jax.ShapeDtypeStruct((8, width + 2 * rim_width + PB), F32),
        in_specs=[VMEM] * 4,
        out_specs=VMEM,
        compiler_params=SMALL,
        name="join",
    )(pair, partner, far, near)
    columns = [column] * shifts
    arrivals = tuple(range(shifts))
    for shift in arrivals[1:]:
        ring = [(i, (i + 2 * shift) % tiles) for i in range(tiles)]
        columns[shift] = lax.ppermute(column, "tile", ring)
    other, own = pair_sums(arrivals, columns, partner, rim)
    step = jnp.concatenate([time_step, step_index.astype(F32)])
    step = jnp.broadcast_to(step[:, None], (2, PB))
    other = lax.ppermute(other, "tile", across)
    return pl.pallas_call(
        advance_kernel,
        out_shape=(
            jax.ShapeDtypeStruct((4, width), F32),
            jax.ShapeDtypeStruct((7, width), F32),
        ),
        in_specs=[VMEM] * 4,
        out_specs=(VMEM, VMEM),
        compiler_params=SMALL,
        name="advance",
    )(step, particles, own(), other)


def solution(mesh):
    placed = (
        P(None, ("slab", "tile")),
        P(("slab", "tile")),
        P(("slab", "tile")),
        P("slab", "tile"),
        P("slab", "tile"),
        P("slab", "tile"),
        P(),
        P(),
    )
    return jax.shard_map(
        on_device,
        mesh=mesh,
        in_specs=placed,
        out_specs=(P(None, ("slab", "tile")), P(None, ("slab", "tile"))),
        check_vma=False,
    )
```
